32 devices in a mesh: blk: 4 (over y, x), head: 8 (over z, core).
Axes of the slice: x: 2, y: 2, z: 4, core: 2. Of those that a mesh axis runs over, the one named last changes fastest.
Arguments:
- tokens: bfloat16 [4, 1024, 2048], P('blk', 'head'), may hold values from -6 to 6
- lengths: int32 [1], replicated, may hold values from 1024 to 4096, as said below
- query_weight: bfloat16 [2048, 2048], P(('blk', 'head')), may hold values from -0.125 to 0.125
- key_weight: bfloat16 [2048, 2048], P(('blk', 'head')), may hold values from -0.125 to 0.125
- value_weight: bfloat16 [2048, 2048], P(('blk', 'head')), may hold values from -0.125 to 0.125
- output_weight: bfloat16 [2048, 2048], P(('blk', 'head')), may hold values from -4 to 4
- gate_weight: bfloat16 [2048, 8192], P(('blk', 'head')), may hold values from -0.125 to 0.125
- up_weight: bfloat16 [2048, 8192], P(('blk', 'head')), may hold values from -0.125 to 0.125
- down_weight: bfloat16 [8192, 2048], P(('blk', 'head')), may hold values from -0.0625 to 0.0625
- cotangent: bfloat16 [4, 1024, 2048], P('blk', 'head'), may hold values from -6 to 6
Outputs:
- layer_output: bfloat16 [4, 1024, 2048], P('blk', 'head')
- tokens_grad: bfloat16 [4, 1024, 2048], P('blk', 'head')
- query_grad: float32 [2048, 2048], P(('blk', 'head'))
- key_grad: float32 [2048, 2048], P(('blk', 'head'))
- value_grad: float32 [2048, 2048], P(('blk', 'head'))
- output_grad: float32 [2048, 2048], P(('blk', 'head'))
- gate_grad: float32 [2048, 8192], P(('blk', 'head'))
- up_grad: float32 [2048, 8192], P(('blk', 'head'))
- down_grad: float32 [8192, 2048], P(('blk', 'head'))
The draws below stay inside these ranges and needn't reach their ends.
Inputs may be any that keep to these rules, and one draw needn't show every extreme that they name: Each slot holds valid tokens at its first lengths positions; in every draw some slot is full.
All inputs are finite; a program needn't handle non-finite values.
Results may differ from the reference program's by a relative error of at most 0.018.
Values may be sent and summed in bfloat16 or wider, within the bound.
No kernel may reach another device: no remote copies, remote signals or barrier semaphores. Data moves between devices by JAX's collectives and lax.ppermute only.
A program may use at most 640 MiB of HBM per device.

```python
import math
import jax
import jax.numpy as jnp
from jax import lax

D = 2048
HEADS = 16
HDIM = 128
FF = 8192
SEQ = 4096
LMIN = 1024
SUB = 1024
SLOTS = 1
N_BLK = 4


def draw_lengths(key, part):
    key = jax.random.fold_in(key, 7)
    first_key, second_key = jax.random.split(key)
    lengths_drawn = jax.random.randint(first_key, (SLOTS,), LMIN, SEQ + 1)
    chosen_slot = jax.random.randint(second_key, (), 0, SLOTS)
    return jnp.where(jnp.arange(SLOTS) == chosen_slot, SEQ, lengths_drawn).astype(jnp.int32)


def levels(stream_key, dims, shards, least, high):
    loudness, own = 1.0, jax.random.fold_in(stream_key, 6)
    for position, parts in shards:
        steps = jnp.exp(jax.random.uniform(jax.random.fold_in(own, position), (parts,), jnp.float32, least / len(shards), high / len(shards)))
        loudness = loudness * jnp.repeat(steps, dims[position] // parts).reshape([-1 if axis == position else 1 for axis in range(len(dims))])
    return loudness


def normal_values(stream_key, dims, scale, most, cuts=(), held_as=jnp.bfloat16):
    drawn = scale * jax.random.normal(stream_key, dims, jnp.float32)
    if cuts:
        drawn = drawn * levels(stream_key, dims, cuts, -0.22, 0.18)
    return jnp.clip(drawn, -most, most).astype(held_as)


def setup_inputs(seed: int = 0) -> dict:
    splits = jax.random.split(jax.random.key(seed), 11)
    return {
        "tokens": normal_values(splits[0], (N_BLK, SLOTS * SUB, D), 1.0, 6.0, ((0, 4), (1, 8))),
        "lengths": draw_lengths(jax.random.fold_in(splits[10], 71), 0),
        "query_weight": normal_values(splits[2], (D, D), D ** -0.5, 0.125, ((0, 32),)),
        "key_weight": normal_values(splits[3], (D, D), D ** -0.5, 0.125, ((0, 32),)),
        "value_weight": normal_values(splits[4], (D, D), D ** -0.5, 0.125, ((0, 32),)),
        "output_weight": normal_values(splits[5], (D, D), (max(1, D * 4 // SEQ)) ** -0.5, 4.0, ((0, 32),)),
        "gate_weight": normal_values(splits[6], (D, FF), D ** -0.5, 0.125, ((0, 32),)),
        "up_weight": normal_values(splits[7], (D, FF), D ** -0.5, 0.125, ((0, 32),)),
        "down_weight": normal_values(splits[8], (FF, D), FF ** -0.5, 0.0625, ((0, 32),)),
        "cotangent": normal_values(splits[9], (N_BLK, SLOTS * SUB, D), 1.0, 6.0, ((0, 4), (1, 8))),
    }


EPSILON = 1e-05
NEGATIVE = -1e+30

@jax.custom_vjp
def low(v):
    return lax.optimization_barrier(v.astype(jnp.bfloat16)).astype(jnp.float32)

@jax.custom_vjp
def low_back(v):
    return v

def low_keep(v):
    return (low(v), None)

def low_pass(kept, grad):
    return (grad,)

def back_keep(v):
    return (v, None)

def back_low(kept, grad):
    return (low(grad),)
low.defvjp(low_keep, low_pass)
low_back.defvjp(back_keep, back_low)

def product(left, right):
    return jnp.dot(left, right, precision=lax.Precision.HIGHEST)

def normalize(values):
    centered = values - lax.optimization_barrier(jnp.mean(values, axis=-1, keepdims=True))
    variance = lax.optimization_barrier(jnp.mean(centered * centered, axis=-1, keepdims=True))
    return centered * lax.rsqrt(variance + EPSILON)

def rotary(values, positions):
    half_dim = HDIM // 2
    frequency = jnp.exp(jnp.arange(half_dim).astype(jnp.float32) * (-2.0 * math.log(10000.0) / HDIM))
    angles = positions.astype(jnp.float32)[:, None] * frequency[None, :]
    cosine_table = jnp.cos(angles)
    sine_table = jnp.sin(angles)
    first_half = values[..., :half_dim]
    second_half = values[..., half_dim:]
    return jnp.concatenate([first_half * cosine_table - second_half * sine_table, second_half * cosine_table + first_half * sine_table], axis=-1)

def head_attention(query_head, key_head, value_head, length):
    positions = jnp.arange(SEQ).astype(jnp.int32)
    query_rot = low(rotary(query_head, positions))
    key_rot = low(rotary(key_head, positions))
    scores = product(query_rot, key_rot.T) * (1.0 / math.sqrt(HDIM))
    visible = (positions[None, :] <= positions[:, None]) & (positions[None, :] < length)
    scores = low_back(jnp.where(visible, scores, NEGATIVE))
    row_peak = lax.optimization_barrier(jnp.max(scores, axis=-1, keepdims=True))
    weights = jnp.exp(scores - row_peak)
    probabilities = low(weights / lax.optimization_barrier(jnp.sum(weights, axis=-1, keepdims=True)))
    return product(probabilities, value_head)

def to_heads(whole_array):
    return whole_array.reshape(SEQ, HEADS, HDIM).transpose(1, 0, 2)

def slot_layer(slot_tokens, length, query_weight, key_weight, value_weight, output_weight, gate_weight, up_weight, down_weight):
    positions = jnp.arange(SEQ).astype(jnp.int32)
    valid_rows = (positions < length).astype(jnp.float32)[:, None]
    normed = low(normalize(slot_tokens))
    queries = low_back(low(product(normed, query_weight)))
    key_act = low_back(low(product(normed, key_weight)))
    values = low_back(low(product(normed, value_weight)))

    def per_head(operands):
        return head_attention(operands[0], operands[1], operands[2], length)
    attended = lax.map(jax.checkpoint(per_head), (to_heads(queries), to_heads(key_act), to_heads(values)))
    joined = low_back(low(attended.transpose(1, 0, 2).reshape(SEQ, D)))
    hidden = slot_tokens + low_back(product(joined, output_weight))
    normed_two = low(normalize(hidden))
    gate_act = low_back(product(normed_two, gate_weight))
    upward = low_back(product(normed_two, up_weight))
    mixed_act = low(jax.nn.silu(gate_act) * upward)
    return (hidden + low_back(product(mixed_act, down_weight))) * valid_rows

def reference(tokens, lengths, query_weight, key_weight, value_weight, output_weight, gate_weight, up_weight, down_weight, cotangent):

    def arrange(whole_array):
        return whole_array.astype(jnp.float32).reshape(N_BLK, SLOTS, SUB, D).transpose(1, 0, 2, 3).reshape(SLOTS, SEQ, D)

    def restore(whole_array):
        return whole_array.reshape(SLOTS, N_BLK, SUB, D).transpose(1, 0, 2, 3).reshape(N_BLK, SLOTS * SUB, D)
    weight_list = tuple((weight_item.astype(jnp.float32) for weight_item in (query_weight, key_weight, value_weight, output_weight, gate_weight, up_weight, down_weight)))

    def forward(slot_inputs, *layer_weights):

        def one_slot(operands):
            return slot_layer(operands[0], operands[1], *layer_weights)
        return lax.map(jax.checkpoint(one_slot), (slot_inputs, lengths))
    result, pullback = jax.vjp(forward, arrange(tokens), *weight_list)
    gradients = pullback(arrange(cotangent))
    return (restore(result).astype(jnp.bfloat16), restore(gradients[0]).astype(jnp.bfloat16), gradients[1], gradients[2], gradients[3], gradients[4], gradients[5], gradients[6], gradients[7])
```

```python
import functools
import math

import jax
import jax.numpy as jnp
from jax import lax
from jax.experimental import pallas as pl
from jax.experimental.pallas import tpu as pltpu
from jax.sharding import PartitionSpec as P

HEADS = 16
HDIM = 128
SEQ = 4096

EPSILON = 1e-05
NEGATIVE = -1e30
SCALE = 1.0 / math.sqrt(HDIM)
VMEM_LIMIT = 48 * 1024 * 1024
BF16 = jnp.bfloat16
F32 = jnp.float32


def normalize_rows(values):
    centered = values - jnp.mean(values, axis=-1, keepdims=True)
    variance = jnp.mean(centered * centered, axis=-1, keepdims=True)
    inverse = lax.rsqrt(variance + EPSILON)
    return (centered * inverse, inverse)


def normalize_back(normed, inverse, upstream):
    mean_grad = jnp.mean(upstream, axis=-1, keepdims=True)
    mean_proj = jnp.mean(upstream * normed, axis=-1, keepdims=True)
    return inverse * (upstream - mean_grad - normed * mean_proj)


def rotary_tables(positions):
    half_dim = HDIM // 2
    frequency = jnp.exp(
        jnp.arange(half_dim).astype(F32) * (-2.0 * math.log(10000.0) / HDIM)
    )
    angles = positions.astype(F32)[:, None] * frequency[None, :]
    cosine, sine = jnp.cos(angles), jnp.sin(angles)
    return (
        jnp.concatenate([cosine, cosine], axis=1),
        jnp.concatenate([-sine, sine], axis=1),
    )


def dot(left, right):
    return jnp.dot(left, right, preferred_element_type=F32)


def dot_transposed(left, right):
    return lax.dot_general(left, right, (((1,), (1,)), ((), ())), preferred_element_type=F32)


def outer_sum(left, right):
    return lax.dot_general(left, right, (((0,), (0,)), ((), ())), preferred_element_type=F32)


def swapped(value, mask, keep=None):
    peers = lax.axis_size("blk")
    pairs = [(i, i ^ mask) for i in range(peers) if keep is None or keep(i, i ^ mask)]
    return lax.ppermute(value, "blk", pairs)


def gather_blk(value):
    peers = lax.axis_size("blk")
    me = lax.axis_index("blk")
    whole = jnp.zeros((peers,) + value.shape, value.dtype)
    whole = lax.dynamic_update_index_in_dim(whole, value, me, 0)
    for mask in range(1, peers):
        whole = lax.dynamic_update_index_in_dim(whole, swapped(value, mask), me ^ mask, 0)
    return whole


def sum_to_owner(part_for):
    peers = lax.axis_size("blk")
    me = lax.axis_index("blk")
    arrived = [
        swapped(part_for(me ^ mask).astype(BF16), mask) for mask in range(1, peers)
    ]
    total = part_for(me)
    for part in arrived:
        total = total + part.astype(F32)
    return total


def rope_kernel(lin_ref, cos_ref, sin_ref, q_ref, kv_ref, *, heads):
    width = heads * HDIM
    cosine, sine = cos_ref[...], sin_ref[...]
    for part in range(2 * heads):
        columns = slice(part * HDIM, (part + 1) * HDIM)
        value = lin_ref[:, columns].astype(F32)
        turned = (value * cosine + pltpu.roll(value, HDIM // 2, 1) * sine).astype(BF16)
        if part < heads:
            q_ref[:, columns] = turned
        else:
            kv_ref[:, slice((part - heads) * HDIM, (part - heads + 1) * HDIM)] = turned
    kv_ref[:, width:] = lin_ref[:, 2 * width :]


def rope(linear, cosine, sine, heads, block_rows):
    rows = linear.shape[0]
    width = heads * HDIM
    tile = min(256, block_rows)
    per_block = block_rows // tile
    return pl.pallas_call(
        functools.partial(rope_kernel, heads=heads),
        grid=(rows // tile,),
        in_specs=[
            pl.BlockSpec((tile, 3 * width), lambda i: (i, 0)),
            pl.BlockSpec((tile, HDIM), lambda i: (i % per_block, 0)),
            pl.BlockSpec((tile, HDIM), lambda i: (i % per_block, 0)),
        ],
        out_specs=[
            pl.BlockSpec((tile, width), lambda i: (i, 0)),
            pl.BlockSpec((tile, 2 * width), lambda i: (i, 0)),
        ],
        out_shape=[
            jax.ShapeDtypeStruct((rows, width), BF16),
            jax.ShapeDtypeStruct((rows, 2 * width), BF16),
        ],
        name="rope",
    )(linear, cosine, sine)


def unrope_kernel(place_ref, dq_ref, cos_ref, sin_ref, *refs, heads, masks):
    parts, out_ref = refs[:-1], refs[-1]
    width = heads * HDIM
    me = place_ref[0]
    cosine, sine = cos_ref[...], sin_ref[...]

    def back(value):
        return (value * cosine - pltpu.roll(value, HDIM // 2, 1) * sine).astype(BF16)

    for head in range(heads):
        columns = slice(head * HDIM, (head + 1) * HDIM)
        out_ref[:, columns] = back(dq_ref[:, columns])
    for part in range(2 * heads):
        columns = slice(part * HDIM, (part + 1) * HDIM)
        total = parts[0][:, columns].astype(F32)
        for mask, ref in zip(masks[1:], parts[1:]):
            total = total + jnp.where((me ^ mask) > me, ref[:, columns].astype(F32), 0.0)
        target = slice(width + part * HDIM, width + (part + 1) * HDIM)
        out_ref[:, target] = back(total) if part < heads else total.astype(BF16)


def unrope(place, dq, cosine, sine, parts, masks, heads, block_rows):
    rows = dq.shape[0]
    width = heads * HDIM
    tile = min(256, block_rows)
    per_block = block_rows // tile
    return pl.pallas_call(
        functools.partial(unrope_kernel, heads=heads, masks=masks),
        grid_spec=pltpu.PrefetchScalarGridSpec(
            num_scalar_prefetch=1,
            grid=(rows // tile,),
            in_specs=[
                pl.BlockSpec((tile, width), lambda i, *_: (i, 0)),
                pl.BlockSpec((tile, HDIM), lambda i, *_: (i % per_block, 0)),
                pl.BlockSpec((tile, HDIM), lambda i, *_: (i % per_block, 0)),
            ]
            + [pl.BlockSpec((tile, 2 * width), lambda i, *_: (i, 0))] * len(parts),
            out_specs=pl.BlockSpec((tile, 3 * width), lambda i, *_: (i, 0)),
        ),
        out_shape=jax.ShapeDtypeStruct((rows, 3 * width), BF16),
        name="unrope",
    )(place, dq, cosine, sine, *parts)


def visible(first_row, rows, first_key, keys, length):
    row = first_row + lax.broadcasted_iota(jnp.int32, (rows, keys), 0)
    key = first_key + lax.broadcasted_iota(jnp.int32, (rows, keys), 1)
    return (key <= row) & (key < length)


def block_cases(place_ref, mask, block_rows, body):
    me = place_ref[0]
    length = place_ref[1 + pl.program_id(0)]
    if mask == 0:
        body(True, True, me, length)
        return
    source = me ^ mask
    whole = (source + 1) * block_rows <= length

    @pl.when((source < me) & whole)
    def _():
        body(False, False, source, length)

    @pl.when((source < me) & jnp.logical_not(whole))
    def _():
        body(False, True, source, length)


def forward_kernel(place_ref, q_ref, *refs, masks, started, final, tile, block_rows):
    kv_refs, refs = refs[: 2 * len(masks)], refs[2 * len(masks) :]
    if started:
        (m_in, l_in, acc_in), refs = refs[:3], refs[3:]
    outs, (m_ref, l_ref, acc_ref) = refs[:-3], refs[-3:]
    if started:
        m_ref[...] = m_in[...]
        l_ref[...] = l_in[...]
        acc_ref[...] = acc_in[...]
    else:
        m_ref[...] = jnp.full(m_ref.shape, NEGATIVE, F32)
        l_ref[...] = jnp.zeros(l_ref.shape, F32)
        acc_ref[...] = jnp.zeros(acc_ref.shape, F32)
    me = place_ref[0]
    for number, mask in enumerate(masks):
        k_ref, v_ref = kv_refs[2 * number], kv_refs[2 * number + 1]

        def body(diagonal, masked, source, length, k_ref=k_ref, v_ref=v_ref):
            for first in range(0, block_rows, tile):
                rows = slice(first, first + tile)
                keys = first + tile if diagonal else block_rows
                scores = dot_transposed(q_ref[rows, :], k_ref[:keys, :]) * SCALE
                if masked:
                    seen = visible(
                        me * block_rows + first, tile, source * block_rows, keys, length
                    )
                    scores = jnp.where(seen, scores, NEGATIVE)
                peak_old = m_ref[rows, :1]
                peak = jnp.maximum(peak_old, jnp.max(scores, axis=1, keepdims=True))
                shrink = jnp.exp(peak_old - peak)
                weights = jnp.exp(scores - peak)
                total = l_ref[rows, :1] * shrink + jnp.sum(weights, axis=1, keepdims=True)
                acc_ref[rows, :] = acc_ref[rows, :] * shrink + dot(
                    weights.astype(BF16), v_ref[:keys, :]
                )
                m_ref[rows, :] = jnp.broadcast_to(peak, (tile, HDIM))
                l_ref[rows, :] = jnp.broadcast_to(total, (tile, HDIM))

        block_cases(place_ref, mask, block_rows, body)
    if final:
        o_ref, lse_ref = outs
        total = l_ref[...]
        o_ref[...] = (acc_ref[...] / total).astype(BF16)
        lse_ref[...] = m_ref[...] + jnp.log(total)
    else:
        for out, ref in zip(outs, (m_ref, l_ref, acc_ref)):
            out[...] = ref[...]


def forward_attention(place, query, blocks, masks, state, final, heads, block_rows):
    rows, width = query.shape
    head_block = pl.BlockSpec((block_rows, HDIM), lambda s, n, *_: (s, n))
    key_block = pl.BlockSpec((block_rows, HDIM), lambda s, n, *_: (s, n))
    value_block = pl.BlockSpec((block_rows, HDIM), lambda s, n, *_: (s, heads + n))
    wide = jax.ShapeDtypeStruct((rows, width), F32)
    outs = [jax.ShapeDtypeStruct((rows, width), BF16), wide] if final else [wide] * 3
    started = state is not None
    operands = [query]
    for block in blocks:
        operands += [block, block]
    operands += list(state) if started else []
    return pl.pallas_call(
        functools.partial(
            forward_kernel,
            masks=masks,
            started=started,
            final=final,
            tile=min(256, block_rows),
            block_rows=block_rows,
        ),
        grid_spec=pltpu.PrefetchScalarGridSpec(
            num_scalar_prefetch=1,
            grid=(rows // block_rows, heads),
            in_specs=[head_block]
            + [key_block, value_block] * len(blocks)
            + ([head_block] * 3 if started else []),
            out_specs=[head_block] * len(outs),
            scratch_shapes=[pltpu.VMEM((block_rows, HDIM), F32)] * 3,
        ),
        out_shape=outs,
        compiler_params=pltpu.CompilerParams(vmem_limit_bytes=VMEM_LIMIT),
        cost_estimate=pl.CostEstimate(
            flops=4 * rows * block_rows * width * len(masks),
            bytes_accessed=4 * rows * width * 8,
            transcendentals=rows * block_rows * heads * len(masks),
        ),
        name="attention_forward",
    )(place, *operands)


def backward_kernel(
    place_ref, q_ref, k_ref, v_ref, o_ref, do_ref, lse_ref, *refs, mask, started, tile, block_rows
):
    if started:
        dq_in, dq_ref, dk_ref, dv_ref, dk_acc, dv_acc = refs
        dq_ref[...] = dq_in[...]
    else:
        dq_ref, dk_ref, dv_ref, dk_acc, dv_acc = refs
        dq_ref[...] = jnp.zeros(dq_ref.shape, F32)
    me = place_ref[0]

    def body(diagonal, masked, source, length):
        dk_acc[...] = jnp.zeros(dk_acc.shape, F32)
        dv_acc[...] = jnp.zeros(dv_acc.shape, F32)
        for first in range(0, block_rows, tile):
            rows = slice(first, first + tile)
            keys = first + tile if diagonal else block_rows
            query, grad = q_ref[rows, :], do_ref[rows, :]
            key, value = k_ref[:keys, :], v_ref[:keys, :]
            delta = jnp.sum(
                grad.astype(F32) * o_ref[rows, :].astype(F32), axis=1, keepdims=True
            )
            scores = dot_transposed(query, key) * SCALE
            if masked:
                seen = visible(me * block_rows + first, tile, source * block_rows, keys, length)
                scores = jnp.where(seen, scores, NEGATIVE)
            probs = jnp.exp(scores - lse_ref[rows, :1])
            dv_acc[:keys, :] += outer_sum(probs.astype(BF16), grad)
            prob_grad = dot_transposed(grad, value)
            score_grad = (probs * (prob_grad - delta)).astype(BF16)
            dk_acc[:keys, :] += outer_sum(score_grad, query)
            dq_ref[rows, :] += dot(score_grad, key) * SCALE
        dk_ref[...] = (dk_acc[...] * SCALE).astype(BF16)
        dv_ref[...] = dv_acc[...].astype(BF16)

    block_cases(place_ref, mask, block_rows, body)


def backward_attention(place, query, block, mask, out, grad, lse, dq, heads, block_rows):
    rows, width = query.shape
    head_block = pl.BlockSpec((block_rows, HDIM), lambda s, n, *_: (s, n))
    value_block = pl.BlockSpec((block_rows, HDIM), lambda s, n, *_: (s, heads + n))
    started = dq is not None
    return pl.pallas_call(
        functools.partial(
            backward_kernel,
            mask=mask,
            started=started,
            tile=min(256, block_rows),
            block_rows=block_rows,
        ),
        grid_spec=pltpu.PrefetchScalarGridSpec(
            num_scalar_prefetch=1,
            grid=(rows // block_rows, heads),
            in_specs=[head_block, head_block, value_block, head_block, head_block, head_block]
            + ([head_block] if started else []),
            out_specs=[head_block] * 3,
            scratch_shapes=[pltpu.VMEM((block_rows, HDIM), F32)] * 2,
        ),
        out_shape=[
            jax.ShapeDtypeStruct((rows, width), F32),
            jax.ShapeDtypeStruct((rows, width), BF16),
            jax.ShapeDtypeStruct((rows, width), BF16),
        ],
        compiler_params=pltpu.CompilerParams(vmem_limit_bytes=VMEM_LIMIT),
        cost_estimate=pl.CostEstimate(
            flops=10 * rows * block_rows * width,
            bytes_accessed=4 * rows * width * 8,
            transcendentals=rows * block_rows * heads,
        ),
        name="attention_backward",
    )(place, query, block, block, out, grad, lse, *([dq] if started else []))


def local(
    tokens,
    lengths,
    query_weight,
    key_weight,
    value_weight,
    output_weight,
    gate_weight,
    up_weight,
    down_weight,
    cotangent,
):
    blocks = lax.axis_size("blk")
    parts = lax.axis_size("head")
    me = lax.axis_index("blk")
    part = lax.axis_index("head")
    inputs = tokens[0].astype(F32)
    token_count, model_width = inputs.shape
    hidden_width = gate_weight.shape[1]
    heads = HEADS // parts
    width = heads * HDIM
    block_rows = SEQ // blocks
    group_rows = token_count * parts
    slots = group_rows // block_rows
    shard_rows = query_weight.shape[0]
    band_rows = shard_rows * parts
    chunk = hidden_width // (blocks * parts)
    masks = list(range(blocks))
    place = jnp.concatenate([me[None].astype(jnp.int32), lengths.astype(jnp.int32)])

    row_ids = part * token_count + jnp.arange(token_count)
    my_length = jnp.sum(
        jnp.where((row_ids // block_rows)[:, None] == jnp.arange(slots)[None, :], lengths[None, :], 0),
        axis=1,
    )
    valid = (me * block_rows + row_ids % block_rows < my_length).astype(F32)[:, None]

    with jax.named_scope("projection_weights"):
        stacked = jnp.stack([query_weight, key_weight, value_weight])
        stacked = stacked.reshape(3, shard_rows, parts, width).transpose(2, 1, 0, 3)
        stacked = lax.all_to_all(stacked, "head", split_axis=0, concat_axis=0, tiled=True)
        projection = gather_blk(stacked.reshape(band_rows, 3 * width)).reshape(
            model_width, 3 * width
        )

    with jax.named_scope("tokens_gather"):
        normed_one, inverse_one = normalize_rows(inputs)
        upstream = cotangent[0].astype(F32) * valid
        upstream_low = upstream.astype(BF16)
        gathered = lax.all_gather(
            jnp.stack([normed_one.astype(BF16), upstream_low]), "head", axis=1, tiled=True
        )
        normed_group, upstream_group = gathered[0], gathered[1]

    with jax.named_scope("hidden_weights"):
        down = gather_blk(down_weight).reshape(blocks * chunk, model_width)
        both = jnp.stack([gate_weight, up_weight]).reshape(2, shard_rows, blocks, parts, chunk)
        both = both.transpose(3, 0, 1, 2, 4)
        both = lax.all_to_all(both, "head", split_axis=0, concat_axis=0, tiled=True)
        both = both.reshape(parts, 2, shard_rows, blocks * chunk)
        gate_band = both[:, 0].reshape(band_rows, blocks * chunk)
        up_band = both[:, 1].reshape(band_rows, blocks * chunk)
        gate = gather_blk(gate_band).reshape(model_width, blocks * chunk)
        up = gather_blk(up_band).reshape(model_width, blocks * chunk)
        output_full = lax.all_gather(output_weight, ("blk", "head"), axis=0, tiled=True)

    cosine, sine = rotary_tables(me * block_rows + jnp.arange(block_rows))
    with jax.named_scope("projections"):
        linear = dot(normed_group, projection).astype(BF16)
        query, key_value = rope(linear, cosine, sine, heads, block_rows)

    with jax.named_scope("attention"):
        sent = [swapped(key_value, mask, lambda i, j: j > i) for mask in masks[1:]]
        state = forward_attention(
            place, query, [key_value], [0], None, False, heads, block_rows
        )
        attended, log_total = forward_attention(
            place, query, sent, masks[1:], state, True, heads, block_rows
        )
        joined = lax.all_to_all(
            attended.reshape(parts, token_count, width), "head", split_axis=0, concat_axis=0, tiled=True
        )
        joined = joined.transpose(1, 0, 2).reshape(token_count, model_width)

    with jax.named_scope("feed_forward"):
        residual = inputs + dot(joined, output_full)
        normed_two, inverse_two = normalize_rows(residual)
        normed_two_group = lax.all_gather(normed_two.astype(BF16), "head", axis=0, tiled=True)
        gate_act = dot(normed_two_group, gate)
        up_act = dot(normed_two_group, up)
        sigmoid_gate = jax.nn.sigmoid(gate_act)
        silu_gate = gate_act * sigmoid_gate
        mixed = (silu_gate * up_act).astype(BF16)
        mixed_grad = dot_transposed(upstream_group, down)
        gate_back = (
            mixed_grad * up_act * sigmoid_gate * (1.0 + gate_act * (1.0 - sigmoid_gate))
        ).astype(BF16)
        up_back = (mixed_grad * silu_gate).astype(BF16)
        normed_two_partial = dot_transposed(gate_back, gate) + dot_transposed(up_back, up)
        normed_two_grad = lax.psum_scatter(
            normed_two_partial.astype(BF16), "head", scatter_dimension=0, tiled=True
        ).astype(F32)
        down_act = lax.psum_scatter(
            dot(mixed, down).astype(BF16), "head", scatter_dimension=0, tiled=True
        ).astype(F32)
        layer_output = ((residual + down_act) * valid).astype(BF16)[None]

    residual_grad = upstream + normalize_back(normed_two, inverse_two, normed_two_grad)
    residual_low = residual_grad.astype(BF16)

    with jax.named_scope("attention_back"):
        joined_grad = dot_transposed(residual_low, output_full).astype(BF16)
        attended_grad = lax.all_to_all(
            joined_grad.reshape(token_count, parts, width).transpose(1, 0, 2),
            "head",
            split_axis=0,
            concat_axis=0,
            tiled=True,
        ).reshape(group_rows, width)
        residual_group = lax.all_gather(residual_low, "head", axis=0, tiled=True)
        query_grad = None
        returned = {}
        for mask in masks[:0:-1] + [0]:
            block = key_value if mask == 0 else sent[mask - 1]
            query_grad, key_part, value_part = backward_attention(
                place, query, block, mask, attended, attended_grad, log_total, query_grad,
                heads, block_rows,
            )
            both_part = jnp.concatenate([key_part, value_part], axis=1)
            returned[mask] = (
                both_part if mask == 0 else swapped(both_part, mask, lambda i, j: j < i)
            )
        projection_back = unrope(
            place, query_grad, cosine, sine, [returned[mask] for mask in masks], masks,
            heads, block_rows,
        )
        normed_one_grad = lax.psum_scatter(
            dot_transposed(projection_back, projection).astype(BF16),
            "head",
            scatter_dimension=0,
            tiled=True,
        ).astype(F32)
        tokens_grad = (
            residual_grad + normalize_back(normed_one, inverse_one, normed_one_grad)
        ).astype(BF16)[None]

    def band(values, place_of):
        return lax.dynamic_slice_in_dim(values, place_of * band_rows, band_rows, 1)

    def to_shards(summed):
        return lax.all_to_all(
            summed.astype(BF16).reshape(parts, shard_rows, summed.shape[1]),
            "head",
            split_axis=0,
            concat_axis=0,
            tiled=True,
        ).astype(F32)

    with jax.named_scope("weight_grads"):
        down_grad = sum_to_owner(
            lambda j: outer_sum(lax.dynamic_slice_in_dim(mixed, j * chunk, chunk, 1), upstream_group)
        )

        def hidden_grad(back):
            summed = sum_to_owner(lambda j: outer_sum(band(normed_two_group, j), back))
            shards = to_shards(summed).reshape(parts, shard_rows, blocks, chunk)
            return shards.transpose(1, 2, 0, 3).reshape(shard_rows, hidden_width)

        gate_grad = hidden_grad(gate_back)
        up_grad = hidden_grad(up_back)
        output_part = sum_to_owner(
            lambda j: outer_sum(
                lax.dynamic_slice_in_dim(attended, j * shard_rows, shard_rows, 1), residual_group
            )
        )
        output_grad = lax.ppermute(
            output_part,
            ("blk", "head"),
            [(b * parts + h, h * blocks + b) for b in range(blocks) for h in range(parts)],
        )
        summed = sum_to_owner(lambda j: outer_sum(band(normed_group, j), projection_back))
        shards = to_shards(summed).reshape(parts, shard_rows, 3, width).transpose(2, 1, 0, 3)
        projection_grads = shards.reshape(3, shard_rows, model_width)
    return (
        layer_output,
        tokens_grad,
        projection_grads[0],
        projection_grads[1],
        projection_grads[2],
        output_grad,
        gate_grad,
        up_grad,
        down_grad,
    )


def solution(mesh):
    rows = P(("blk", "head"), None)
    places = P("blk", "head", None)
    in_specs = (places, P(), rows, rows, rows, rows, rows, rows, rows, places)
    out_specs = (places, places, rows, rows, rows, rows, rows, rows, rows)
    return jax.shard_map(local, mesh=mesh, in_specs=in_specs, out_specs=out_specs, check_vma=False)
```

```python
import functools
import math

import jax
import jax.numpy as jnp
from jax import lax
from jax.experimental import pallas as pl
from jax.experimental.pallas import tpu as pltpu
from jax.sharding import PartitionSpec as P

HEADS = 16
HDIM = 128
SEQ = 4096

EPSILON = 1e-05
NEGATIVE = -1e30
SCALE = 1.0 / math.sqrt(HDIM)
SCALE2 = SCALE * math.log2(math.e)
TILE = 512
VMEM_LIMIT = 48 * 1024 * 1024
BF16 = jnp.bfloat16
F32 = jnp.float32


def normalize_rows(values):
    centered = values - jnp.mean(values, axis=-1, keepdims=True)
    variance = jnp.mean(centered * centered, axis=-1, keepdims=True)
    inverse = lax.rsqrt(variance + EPSILON)
    return (centered * inverse, inverse)


def normalize_back(normed, inverse, upstream):
    mean_grad = jnp.mean(upstream, axis=-1, keepdims=True)
    mean_proj = jnp.mean(upstream * normed, axis=-1, keepdims=True)
    return inverse * (upstream - mean_grad - normed * mean_proj)


def rotary_tables(positions):
    half_dim = HDIM // 2
    frequency = jnp.exp(
        jnp.arange(half_dim).astype(F32) * (-2.0 * math.log(10000.0) / HDIM)
    )
    angles = positions.astype(F32)[:, None] * frequency[None, :]
    cosine, sine = jnp.cos(angles), jnp.sin(angles)
    return (
        jnp.concatenate([cosine, cosine], axis=1),
        jnp.concatenate([-sine, sine], axis=1),
    )


def dot(left, right):
    return jnp.dot(left, right, preferred_element_type=F32)


def dot_transposed(left, right):
    return lax.dot_general(left, right, (((1,), (1,)), ((), ())), preferred_element_type=F32)


def outer_sum(left, right):
    return lax.dot_general(left, right, (((0,), (0,)), ((), ())), preferred_element_type=F32)


def swapped(value, mask, keep=None):
    peers = lax.axis_size("blk")
    pairs = [(i, i ^ mask) for i in range(peers) if keep is None or keep(i, i ^ mask)]
    return lax.ppermute(value, "blk", pairs)


def after(value, *others):
    return lax.optimization_barrier((value,) + others)[0]


def send_near(value):
    peers = lax.axis_size("blk")
    return [swapped(value, mask) for mask in range(1, 3 if peers == 4 else peers)]


def send_far(near):
    if lax.axis_size("blk") != 4:
        return []
    first, second = near
    half = first.shape[0] // 2
    return [[swapped(first[:half], 2), swapped(second[half:], 1)]]


def gather_blk(value, arrived):
    peers = lax.axis_size("blk")
    me = lax.axis_index("blk")
    whole = jnp.zeros((peers,) + value.shape, value.dtype)
    whole = lax.dynamic_update_index_in_dim(whole, value, me, 0)
    for mask, part in enumerate(arrived, 1):
        row = 0
        for piece in part if isinstance(part, list) else [part]:
            start = (me ^ mask, row) + (0,) * (value.ndim - 1)
            whole = lax.dynamic_update_slice(whole, piece[None], start)
            row += piece.shape[0]
    return whole


def terms_of(part_for):
    peers = lax.axis_size("blk")
    me = lax.axis_index("blk")
    return [part_for(me)] + [part_for(me ^ mask).astype(BF16) for mask in range(1, peers)]


def near_halves(terms):
    half = terms[0].shape[0] // 2
    return ((slice(0, half), 1, 2), (slice(half, None), 2, 1))


def sum_pass(terms):
    if len(terms) != 4:
        return []
    return [swapped(terms[3][rows], near) for rows, near, _ in near_halves(terms)]


def sum_own(terms):
    if len(terms) != 4:
        return [swapped(term, mask) for mask, term in enumerate(terms) if mask]
    return [swapped(terms[near][rows], near) for rows, near, _ in near_halves(terms)]


def sum_far(terms, passed):
    return [
        swapped((terms[far][rows].astype(F32) + part.astype(F32)).astype(BF16), far)
        for part, (rows, _, far) in zip(passed, near_halves(terms))
    ]


def sum_end(terms, own, far):
    total = terms[0]
    if len(terms) != 4:
        for part in own:
            total = total + part.astype(F32)
        return total
    totals = [
        total[rows] + first.astype(F32) + second.astype(F32)
        for first, second, (rows, _, _) in zip(own, far, near_halves(terms))
    ]
    return jnp.concatenate(totals, axis=0)


def sum_to_owner(terms):
    return sum_end(terms, sum_own(terms), sum_far(terms, sum_pass(terms)))


def collect_kernel(*refs, parts, blocks, chunk):
    *ins, out_ref = refs
    for number, ref in enumerate(ins):
        for block in range(blocks):
            first = (number * blocks + block) * chunk
            for part in range(parts):
                start = (block * parts + part) * chunk
                out_ref[part, :, first : first + chunk] = ref[:, start : start + chunk]


def collect(arrays, parts, blocks, chunk):
    rows = arrays[0].shape[0]
    return pl.pallas_call(
        functools.partial(collect_kernel, parts=parts, blocks=blocks, chunk=chunk),
        out_shape=jax.ShapeDtypeStruct(
            (parts, rows, len(arrays) * blocks * chunk), arrays[0].dtype
        ),
        compiler_params=pltpu.CompilerParams(vmem_limit_bytes=VMEM_LIMIT),
        name="collect",
    )(*arrays)


def spread_kernel(in_ref, *outs, parts, blocks, chunk):
    for number, ref in enumerate(outs):
        for block in range(blocks):
            first = (number * blocks + block) * chunk
            for part in range(parts):
                start = (block * parts + part) * chunk
                ref[:, start : start + chunk] = in_ref[part, :, first : first + chunk].astype(F32)


def spread(array, count, parts, blocks, chunk):
    rows = array.shape[1]
    shape = jax.ShapeDtypeStruct((rows, blocks * parts * chunk), F32)
    return pl.pallas_call(
        functools.partial(spread_kernel, parts=parts, blocks=blocks, chunk=chunk),
        out_shape=[shape] * count,
        compiler_params=pltpu.CompilerParams(vmem_limit_bytes=VMEM_LIMIT),
        name="spread",
    )(array)


def rope_kernel(lin_ref, cos_ref, sin_ref, q_ref, kv_ref, *, heads):
    width = heads * HDIM
    cosine, sine = cos_ref[...], sin_ref[...]
    for part in range(2 * heads):
        columns = slice(part * HDIM, (part + 1) * HDIM)
        value = lin_ref[:, columns].astype(F32)
        turned = (value * cosine + pltpu.roll(value, HDIM // 2, 1) * sine).astype(BF16)
        if part < heads:
            q_ref[:, columns] = turned
        else:
            start = 2 * (part - heads) * HDIM
            kv_ref[:, start : start + HDIM] = turned
            columns = slice((part + heads) * HDIM, (part + heads + 1) * HDIM)
            kv_ref[:, start + HDIM : start + 2 * HDIM] = lin_ref[:, columns]


def rope(linear, cosine, sine, heads, block_rows):
    rows = linear.shape[0]
    width = heads * HDIM
    tile = min(256, block_rows)
    per_block = block_rows // tile
    return pl.pallas_call(
        functools.partial(rope_kernel, heads=heads),
        grid=(rows // tile,),
        in_specs=[
            pl.BlockSpec((tile, 3 * width), lambda i: (i, 0)),
            pl.BlockSpec((tile, HDIM), lambda i: (i % per_block, 0)),
            pl.BlockSpec((tile, HDIM), lambda i: (i % per_block, 0)),
        ],
        out_specs=[
            pl.BlockSpec((tile, width), lambda i: (i, 0)),
            pl.BlockSpec((tile, 2 * width), lambda i: (i, 0)),
        ],
        out_shape=[
            jax.ShapeDtypeStruct((rows, width), BF16),
            jax.ShapeDtypeStruct((rows, 2 * width), BF16),
        ],
        name="rope",
    )(linear, cosine, sine)


def unrope_kernel(place_ref, dq_ref, cos_ref, sin_ref, *refs, heads, masks):
    parts, out_ref = refs[:-1], refs[-1]
    width = heads * HDIM
    me = place_ref[0]
    cosine, sine = cos_ref[...], sin_ref[...]

    def back(value):
        return (value * cosine - pltpu.roll(value, HDIM // 2, 1) * sine).astype(BF16)

    for head in range(heads):
        columns = slice(head * HDIM, (head + 1) * HDIM)
        out_ref[:, columns] = back(dq_ref[:, columns])
    for part in range(2 * heads):
        head, is_value = part // 2, part % 2
        columns = slice(part * HDIM, (part + 1) * HDIM)
        total = parts[0][:, columns].astype(F32)
        for mask, ref in zip(masks[1:], parts[1:]):
            total = total + jnp.where((me ^ mask) > me, ref[:, columns].astype(F32), 0.0)
        start = (1 + is_value) * width + head * HDIM
        out_ref[:, start : start + HDIM] = total.astype(BF16) if is_value else back(total)


def unrope(place, dq, cosine, sine, parts, masks, heads, block_rows):
    rows = dq.shape[0]
    width = heads * HDIM
    tile = min(256, block_rows)
    per_block = block_rows // tile
    return pl.pallas_call(
        functools.partial(unrope_kernel, heads=heads, masks=masks),
        grid_spec=pltpu.PrefetchScalarGridSpec(
            num_scalar_prefetch=1,
            grid=(rows // tile,),
            in_specs=[
                pl.BlockSpec((tile, width), lambda i, *_: (i, 0)),
                pl.BlockSpec((tile, HDIM), lambda i, *_: (i % per_block, 0)),
                pl.BlockSpec((tile, HDIM), lambda i, *_: (i % per_block, 0)),
            ]
            + [pl.BlockSpec((tile, 2 * width), lambda i, *_: (i, 0))] * len(parts),
            out_specs=pl.BlockSpec((tile, 3 * width), lambda i, *_: (i, 0)),
        ),
        out_shape=jax.ShapeDtypeStruct((rows, 3 * width), BF16),
        name="unrope",
    )(place, dq, cosine, sine, *parts)


def visible(first_row, rows, first_key, keys, length):
    row = first_row + lax.broadcasted_iota(jnp.int32, (keys, rows), 1)
    key = first_key + lax.broadcasted_iota(jnp.int32, (keys, rows), 0)
    return (key <= row) & (key < length)

def block_cases(place_ref, mask, block_rows, body):
    me = place_ref[0]
    length = place_ref[1 + pl.program_id(0)]
    if mask == 0:
        body(True, True, me, length)
        return
    source = me ^ mask
    whole = (source + 1) * block_rows <= length
    @pl.when((source < me) & whole)
    def _():
        body(False, False, source, length)
    @pl.when((source < me) & jnp.logical_not(whole))
    def _():
        body(False, True, source, length)

def forward_kernel(place_ref, q_ref, *refs, masks, started, final, tile, block_rows):
    kv_refs, refs = refs[: len(masks)], refs[len(masks) :]
    if started:
        (m_in, l_in, acc_in), refs = refs[:3], refs[3:]
    outs, (m_ref, l_ref, acc_ref) = refs[:-3], refs[-3:]
    if started:
        m_ref[...] = m_in[0]
        l_ref[...] = l_in[0]
        acc_ref[...] = acc_in[0]
    else:
        m_ref[...] = jnp.full(m_ref.shape, NEGATIVE, F32)
        l_ref[...] = jnp.zeros(l_ref.shape, F32)
        acc_ref[...] = jnp.zeros(acc_ref.shape, F32)
    me = place_ref[0]
    for mask, kv_ref in zip(masks, kv_refs):

        def body(diagonal, masked, source, length, kv_ref=kv_ref):
            for first in range(0, block_rows, tile):
                rows = slice(first, first + tile)
                keys = first + tile if diagonal else block_rows
                scores = dot_transposed(kv_ref[:keys, :HDIM], q_ref[rows, :])
                if masked:
                    seen = visible(me * block_rows + first, tile, source * block_rows, keys, length)
                    scores = jnp.where(seen, scores, NEGATIVE)
                peak_old = m_ref[:, rows]
                peak = jnp.maximum(peak_old, jnp.max(scores, axis=0, keepdims=True) * SCALE2)
                shrink = jnp.exp2(peak_old - peak)
                weights = jnp.exp2(scores * SCALE2 - peak)
                l_ref[:, rows] = l_ref[:, rows] * shrink + jnp.sum(weights, axis=0, keepdims=True)
                acc_ref[:, rows] = acc_ref[:, rows] * shrink + outer_sum(
                    kv_ref[:keys, HDIM:], weights.astype(BF16)
                )
                m_ref[:, rows] = peak
        block_cases(place_ref, mask, block_rows, body)
    if final:
        o_ref, lse_ref = outs
        total = l_ref[...]
        o_ref[...] = (acc_ref[...] / total).T.astype(BF16)
        lse_ref[0] = m_ref[...] + jnp.log2(total)
    else:
        for out, ref in zip(outs, (m_ref, l_ref, acc_ref)):
            out[0] = ref[...]

def forward_attention(place, query, blocks, masks, state, final, heads, block_rows):
    rows, width = query.shape
    groups = rows // block_rows * heads
    head_block = pl.BlockSpec((block_rows, HDIM), lambda s, n, *_: (s, n))
    pair_block = pl.BlockSpec((block_rows, 2 * HDIM), lambda s, n, *_: (s, n))
    row_block = pl.BlockSpec((1, 1, block_rows), lambda s, n, *_: (s * heads + n, 0, 0))
    acc_block = pl.BlockSpec((1, HDIM, block_rows), lambda s, n, *_: (s * heads + n, 0, 0))
    row_shape = jax.ShapeDtypeStruct((groups, 1, block_rows), F32)
    acc_shape = jax.ShapeDtypeStruct((groups, HDIM, block_rows), F32)
    if final:
        out_specs, out_shape = [head_block, row_block], [jax.ShapeDtypeStruct((rows, width), BF16), row_shape]
    else:
        out_specs, out_shape = [row_block, row_block, acc_block], [row_shape, row_shape, acc_shape]
    started = state is not None
    operands = [query, *blocks] + (list(state) if started else [])
    return pl.pallas_call(
        functools.partial(forward_kernel, masks=masks, started=started, final=final, tile=min(TILE, block_rows), block_rows=block_rows),
        grid_spec=pltpu.PrefetchScalarGridSpec(
            num_scalar_prefetch=1, grid=(rows // block_rows, heads),
            in_specs=[head_block] + [pair_block] * len(blocks) + ([row_block, row_block, acc_block] if started else []),
            out_specs=out_specs,
            scratch_shapes=[pltpu.VMEM((1, block_rows), F32)] * 2 + [pltpu.VMEM((HDIM, block_rows), F32)],
        ),
        out_shape=out_shape,
        compiler_params=pltpu.CompilerParams(vmem_limit_bytes=VMEM_LIMIT),
        name="attention_forward",
    )(place, *operands)

def backward_kernel(
    place_ref, q_ref, o_ref, do_ref, lse_ref, *refs, masks, started, final, tile, block_rows
):
    kv_refs, refs = refs[: len(masks)], refs[len(masks) :]
    if started:
        dq_in, refs = refs[0], refs[1:]
    dq_ref, dkv_refs, (dq_acc, dk_acc, dv_acc) = refs[0], refs[1:-3], refs[-3:]
    dq_acc[...] = dq_in[0] if started else jnp.zeros(dq_acc.shape, F32)
    me = place_ref[0]
    for mask, kv_ref, dkv_ref in zip(masks, kv_refs, dkv_refs):

        def body(diagonal, masked, source, length, kv_ref=kv_ref, dkv_ref=dkv_ref):
            for first in range(0, block_rows, tile):
                rows = slice(first, first + tile)
                keys = first + tile if diagonal else block_rows
                query, grad = q_ref[rows, :], do_ref[rows, :]
                key, value = kv_ref[:keys, :HDIM], kv_ref[:keys, HDIM:]
                delta = jnp.sum(
                    (grad.astype(F32) * o_ref[rows, :].astype(F32)).T, axis=0, keepdims=True
                )
                scores = dot_transposed(key, query)
                if masked:
                    seen = visible(
                        me * block_rows + first, tile, source * block_rows, keys, length
                    )
                    scores = jnp.where(seen, scores, NEGATIVE)
                probs = jnp.exp2(scores * SCALE2 - lse_ref[0, :, rows])
                prob_grad = dot_transposed(value, grad)
                score_grad = (probs * (prob_grad - delta)).astype(BF16)
                dv = dot(probs.astype(BF16), grad)
                dk = dot(score_grad, query)
                dq_acc[:, rows] += outer_sum(key, score_grad) * SCALE
                if diagonal:
                    if first:
                        dk_acc[:first, :] += dk[:first]
                        dv_acc[:first, :] += dv[:first]
                    dk_acc[rows, :] = dk[first:]
                    dv_acc[rows, :] = dv[first:]
                elif first == 0:
                    dk_acc[...] = dk
                    dv_acc[...] = dv
                else:
                    dk_acc[...] += dk
                    dv_acc[...] += dv
            dkv_ref[:, :HDIM] = (dk_acc[...] * SCALE).astype(BF16)
            dkv_ref[:, HDIM:] = dv_acc[...].astype(BF16)

        block_cases(place_ref, mask, block_rows, body)
    if final:
        dq_ref[...] = dq_acc[...].T
    else:
        dq_ref[0] = dq_acc[...]


def backward_attention(
    place, query, blocks, masks, out, grad, lse, dq, final, heads, block_rows
):
    rows, width = query.shape
    groups = rows // block_rows * heads
    head_block = pl.BlockSpec((block_rows, HDIM), lambda s, n, *_: (s, n))
    pair_block = pl.BlockSpec((block_rows, 2 * HDIM), lambda s, n, *_: (s, n))
    row_block = pl.BlockSpec((1, 1, block_rows), lambda s, n, *_: (s * heads + n, 0, 0))
    acc_block = pl.BlockSpec((1, HDIM, block_rows), lambda s, n, *_: (s * heads + n, 0, 0))
    started = dq is not None
    if final:
        dq_shape = jax.ShapeDtypeStruct((rows, width), F32)
    else:
        dq_shape = jax.ShapeDtypeStruct((groups, HDIM, block_rows), F32)
    dkv_shape = jax.ShapeDtypeStruct((rows, 2 * width), BF16)
    return pl.pallas_call(
        functools.partial(
            backward_kernel,
            masks=masks,
            started=started,
            final=final,
            tile=min(TILE, block_rows),
            block_rows=block_rows,
        ),
        grid_spec=pltpu.PrefetchScalarGridSpec(
            num_scalar_prefetch=1,
            grid=(rows // block_rows, heads),
            in_specs=[head_block] * 3
            + [row_block]
            + [pair_block] * len(masks)
            + ([acc_block] if started else []),
            out_specs=[head_block if final else acc_block] + [pair_block] * len(masks),
            scratch_shapes=[pltpu.VMEM((HDIM, block_rows), F32)]
            + [pltpu.VMEM((block_rows, HDIM), F32)] * 2,
        ),
        out_shape=[dq_shape] + [dkv_shape] * len(masks),
        compiler_params=pltpu.CompilerParams(vmem_limit_bytes=VMEM_LIMIT),
        name="attention_backward",
    )(place, query, out, grad, lse, *blocks, *([dq] if started else []))


def local(
    tokens,
    lengths,
    query_weight,
    key_weight,
    value_weight,
    output_weight,
    gate_weight,
    up_weight,
    down_weight,
    cotangent,
):
    blocks = lax.axis_size("blk")
    parts = lax.axis_size("head")
    me = lax.axis_index("blk")
    part = lax.axis_index("head")
    inputs = tokens[0].astype(F32)
    token_count, model_width = inputs.shape
    hidden_width = gate_weight.shape[1]
    heads = HEADS // parts
    width = heads * HDIM
    block_rows = SEQ // blocks
    group_rows = token_count * parts
    slots = group_rows // block_rows
    shard_rows = query_weight.shape[0]
    band_rows = shard_rows * parts
    chunk = hidden_width // (blocks * parts)
    masks = list(range(blocks))
    place = jnp.concatenate([me[None].astype(jnp.int32), lengths.astype(jnp.int32)])

    row_ids = part * token_count + jnp.arange(token_count)
    my_length = jnp.sum(
        jnp.where((row_ids // block_rows)[:, None] == jnp.arange(slots)[None, :], lengths[None, :], 0),
        axis=1,
    )
    valid = (me * block_rows + row_ids % block_rows < my_length).astype(F32)[:, None]

    with jax.named_scope("projection_weights"):
        stacked = collect([query_weight, key_weight, value_weight], parts, 1, width)
        stacked = lax.all_to_all(stacked, "head", split_axis=0, concat_axis=0, tiled=True)
        stacked = stacked.reshape(band_rows, 3 * width)
        down_near = send_near(down_weight)
        output_rows = lax.ppermute(
            output_weight,
            ("blk", "head"),
            [(h * blocks + b, b * parts + h) for b in range(blocks) for h in range(parts)],
        )
        stacked, down_near, output_rows = lax.optimization_barrier(
            (stacked, down_near, output_rows)
        )
        near = send_near(stacked)
        projection = gather_blk(stacked, near + send_far(near)).reshape(model_width, 3 * width)

    with jax.named_scope("tokens_gather"):
        normed_one, inverse_one = normalize_rows(inputs)
        upstream = cotangent[0].astype(F32) * valid
        upstream_low = upstream.astype(BF16)
        normed_group = lax.all_gather(
            after(normed_one.astype(BF16), stacked), "head", axis=0, tiled=True
        )

    with jax.named_scope("hidden_weights"):
        both = collect([gate_weight, up_weight], parts, blocks, chunk)
        normed_group, projection = lax.optimization_barrier((normed_group, projection))

    cosine, sine = rotary_tables(me * block_rows + jnp.arange(block_rows))
    with jax.named_scope("projections"):
        linear = dot(normed_group, projection).astype(BF16)
        query, key_value = rope(linear, cosine, sine, heads, block_rows)

    with jax.named_scope("attention"):
        sent = [swapped(key_value, mask, lambda i, j: j > i) for mask in masks[1:]]
        state = forward_attention(
            place, query, [key_value], [0], None, False, heads, block_rows
        )
        both = lax.all_to_all(
            after(both, normed_group), "head", split_axis=0, concat_axis=0, tiled=True
        ).reshape(band_rows, 2 * blocks * chunk)
        output_near = send_near(after(output_rows, key_value))
        output = gather_blk(output_rows, output_near + send_far(output_near))
        output = output.reshape(width, model_width)
        upstream_group = lax.all_gather(
            after(upstream_low, normed_group), "head", axis=0, tiled=True
        )
        state, sent, both, output, upstream_group = lax.optimization_barrier(
            (state, sent, both, output, upstream_group)
        )
        near, down_far = send_near(both), send_far(down_near)
        attended, log_total = forward_attention(
            place, query, sent, masks[1:], state, True, heads, block_rows
        )
        joined = lax.psum_scatter(
            dot(attended, output).astype(BF16), "head", scatter_dimension=0, tiled=True
        )
        joined, near = lax.optimization_barrier((joined, near))
        both = gather_blk(both, near + send_far(near)).reshape(model_width, 2 * blocks * chunk)
        down = gather_blk(down_weight, down_near + down_far).reshape(blocks * chunk, model_width)

    with jax.named_scope("feed_forward"):
        residual = inputs + joined.astype(F32)
        normed_two, inverse_two = normalize_rows(residual)
        normed_two_group = lax.all_gather(normed_two.astype(BF16), "head", axis=0, tiled=True)
        both_act = dot(normed_two_group, both)
        gate_act, up_act = jnp.split(both_act, 2, axis=1)
        sigmoid_gate = jax.nn.sigmoid(gate_act)
        silu_gate = gate_act * sigmoid_gate
        mixed = (silu_gate * up_act).astype(BF16)
        mixed_grad = dot_transposed(upstream_group, down)
        gate_back = (
            mixed_grad * up_act * sigmoid_gate * (1.0 + gate_act * (1.0 - sigmoid_gate))
        ).astype(BF16)
        up_back = (mixed_grad * silu_gate).astype(BF16)
        both_back = jnp.concatenate([gate_back, up_back], axis=1)
        normed_two_partial = dot_transposed(both_back, both)
        normed_two_grad = lax.psum_scatter(
            normed_two_partial.astype(BF16), "head", scatter_dimension=0, tiled=True
        ).astype(F32)
        down_partial = dot(mixed, down).astype(BF16)

        def band(values, place_of):
            return lax.dynamic_slice_in_dim(values, place_of * band_rows, band_rows, 1)

        both_terms = terms_of(lambda j: outer_sum(band(normed_two_group, j), both_back))
        both_passed = sum_pass(both_terms)
        down_terms = terms_of(
            lambda j: outer_sum(lax.dynamic_slice_in_dim(mixed, j * chunk, chunk, 1), upstream_group)
        )
        normed_two_grad, down_partial, both_terms, both_passed, down_terms = (
            lax.optimization_barrier(
                (normed_two_grad, down_partial, both_terms, both_passed, down_terms)
            )
        )

    residual_grad = upstream + normalize_back(normed_two, inverse_two, normed_two_grad)
    residual_low = residual_grad.astype(BF16)

    def to_shards(summed):
        return lax.all_to_all(
            summed.astype(BF16).reshape(parts, shard_rows, summed.shape[1]),
            "head",
            split_axis=0,
            concat_axis=0,
            tiled=True,
        )

    with jax.named_scope("attention_back"):
        residual_group = lax.all_gather(residual_low, "head", axis=0, tiled=True)
        both_own, both_far = sum_own(both_terms), sum_far(both_terms, both_passed)
        down_passed = sum_pass(down_terms)
        residual_group, both_own, both_far, down_terms, down_passed = lax.optimization_barrier(
            (residual_group, both_own, both_far, down_terms, down_passed)
        )
        both_sum = sum_end(both_terms, both_own, both_far)
        attended_grad = dot_transposed(residual_group, output).astype(BF16)
        down_act = lax.psum_scatter(
            after(down_partial, residual_group), "head", scatter_dimension=0, tiled=True
        ).astype(F32)
        query_grad, *remote = backward_attention(
            place, query, sent, masks[1:], attended, attended_grad, log_total, None,
            False, heads, block_rows,
        )
        returned = [
            swapped(part, mask, lambda i, j: j < i) for mask, part in zip(masks[1:], remote)
        ]
        hidden_shards = to_shards(both_sum)
        query_grad, returned, hidden_shards = lax.optimization_barrier(
            (query_grad, returned, hidden_shards)
        )
        query_grad, own = backward_attention(
            place, query, [key_value], [0], attended, attended_grad, log_total, query_grad,
            True, heads, block_rows,
        )
        down_sum = sum_end(down_terms, sum_own(down_terms), sum_far(down_terms, down_passed))
        output_terms = terms_of(
            lambda j: outer_sum(
                lax.dynamic_slice_in_dim(attended, j * shard_rows, shard_rows, 1), residual_group
            )
        )
        output_grad = lax.ppermute(
            sum_to_owner(output_terms).astype(BF16),
            ("blk", "head"),
            [(b * parts + h, h * blocks + b) for b in range(blocks) for h in range(parts)],
        ).astype(F32)
        down_act = after(down_act, query_grad)
        layer_output = ((residual + down_act) * valid).astype(BF16)[None]
        projection_back = unrope(
            place, query_grad, cosine, sine, [own] + returned, masks,
            heads, block_rows,
        )
        normed_one_grad = lax.psum_scatter(
            dot_transposed(projection_back, projection).astype(BF16),
            "head",
            scatter_dimension=0,
            tiled=True,
        ).astype(F32)
        tokens_grad = (
            residual_grad + normalize_back(normed_one, inverse_one, normed_one_grad)
        ).astype(BF16)[None]

    with jax.named_scope("weight_grads"):

        gate_grad, up_grad = spread(hidden_shards, 2, parts, blocks, chunk)
        summed = sum_to_owner(terms_of(lambda j: outer_sum(band(normed_group, j), projection_back)))
        projection_grads = spread(to_shards(summed), 3, parts, 1, width)
    return (
        layer_output,
        tokens_grad,
        projection_grads[0],
        projection_grads[1],
        projection_grads[2],
        output_grad,
        gate_grad,
        up_grad,
        down_sum,
    )


def solution(mesh):
    rows = P(("blk", "head"), None)
    places = P("blk", "head", None)
    in_specs = (places, P(), rows, rows, rows, rows, rows, rows, rows, places)
    out_specs = (places, places, rows, rows, rows, rows, rows, rows, rows)
    return jax.shard_map(local, mesh=mesh, in_specs=in_specs, out_specs=out_specs, check_vma=False)
```

```python
import functools
import math

import jax
import jax.numpy as jnp
from jax import lax
from jax.experimental import pallas as pl
from jax.experimental.pallas import tpu as pltpu
from jax.sharding import PartitionSpec as P

HEADS = 16
HDIM = 128
SEQ = 4096

EPSILON = 1e-05
NEGATIVE = -1e30
SCALE = 1.0 / math.sqrt(HDIM)
SCALE2 = SCALE * math.log2(math.e)
TILE = 512
VMEM_LIMIT = 48 * 1024 * 1024
BF16 = jnp.bfloat16
F32 = jnp.float32


def normalize_rows(values):
    centered = values - jnp.mean(values, axis=-1, keepdims=True)
    variance = jnp.mean(centered * centered, axis=-1, keepdims=True)
    inverse = lax.rsqrt(variance + EPSILON)
    return (centered * inverse, inverse)


def normalize_back(normed, inverse, upstream):
    mean_grad = jnp.mean(upstream, axis=-1, keepdims=True)
    mean_proj = jnp.mean(upstream * normed, axis=-1, keepdims=True)
    return inverse * (upstream - mean_grad - normed * mean_proj)


def rotary_tables(positions):
    half_dim = HDIM // 2
    frequency = jnp.exp(
        jnp.arange(half_dim).astype(F32) * (-2.0 * math.log(10000.0) / HDIM)
    )
    angles = positions.astype(F32)[:, None] * frequency[None, :]
    cosine, sine = jnp.cos(angles), jnp.sin(angles)
    return (
        jnp.concatenate([cosine, cosine], axis=1),
        jnp.concatenate([-sine, sine], axis=1),
    )


def dot(left, right):
    return jnp.dot(left, right, preferred_element_type=F32)


def dot_transposed(left, right):
    return lax.dot_general(left, right, (((1,), (1,)), ((), ())), preferred_element_type=F32)


def outer_sum(left, right):
    return lax.dot_general(left, right, (((0,), (0,)), ((), ())), preferred_element_type=F32)


def swapped(value, mask, keep=None):
    peers = lax.axis_size("blk")
    pairs = [(i, i ^ mask) for i in range(peers) if keep is None or keep(i, i ^ mask)]
    return lax.ppermute(value, "blk", pairs)


def after(value, *others):
    return lax.optimization_barrier((value,) + others)[0]


def send_near(value):
    peers = lax.axis_size("blk")
    return [swapped(value, mask) for mask in range(1, 3 if peers == 4 else peers)]


def send_far(near):
    if lax.axis_size("blk") != 4:
        return []
    first, second = near
    half = first.shape[0] // 2
    return [[swapped(first[:half], 2), swapped(second[half:], 1)]]


def gather_blk(value, arrived):
    peers = lax.axis_size("blk")
    me = lax.axis_index("blk")
    whole = jnp.zeros((peers,) + value.shape, value.dtype)
    whole = lax.dynamic_update_index_in_dim(whole, value, me, 0)
    for mask, part in enumerate(arrived, 1):
        row = 0
        for piece in part if isinstance(part, list) else [part]:
            start = (me ^ mask, row) + (0,) * (value.ndim - 1)
            whole = lax.dynamic_update_slice(whole, piece[None], start)
            row += piece.shape[0]
    return whole


def terms_of(part_for):
    peers = lax.axis_size("blk")
    me = lax.axis_index("blk")
    return [part_for(me)] + [part_for(me ^ mask).astype(BF16) for mask in range(1, peers)]


def near_halves(terms):
    half = terms[0].shape[0] // 2
    return ((slice(0, half), 1, 2), (slice(half, None), 2, 1))


def sum_pass(terms):
    if len(terms) != 4:
        return []
    return [swapped(terms[3][rows], near) for rows, near, _ in near_halves(terms)]


def sum_own(terms):
    if len(terms) != 4:
        return [swapped(term, mask) for mask, term in enumerate(terms) if mask]
    return [swapped(terms[near][rows], near) for rows, near, _ in near_halves(terms)]


def sum_far(terms, passed):
    return [
        swapped((terms[far][rows].astype(F32) + part.astype(F32)).astype(BF16), far)
        for part, (rows, _, far) in zip(passed, near_halves(terms))
    ]


def sum_end(terms, own, far):
    total = terms[0]
    if len(terms) != 4:
        for part in own:
            total = total + part.astype(F32)
        return total
    totals = [
        total[rows] + first.astype(F32) + second.astype(F32)
        for first, second, (rows, _, _) in zip(own, far, near_halves(terms))
    ]
    return jnp.concatenate(totals, axis=0)


def sum_to_owner(terms):
    arrived = [swapped(term, mask) for mask, term in enumerate(terms) if mask]
    total = terms[0]
    for part in arrived:
        total = total + part.astype(F32)
    return total


def collect_kernel(*refs, parts, blocks, chunk):
    *ins, out_ref = refs
    for number, ref in enumerate(ins):
        for block in range(blocks):
            first = (number * blocks + block) * chunk
            for part in range(parts):
                start = (block * parts + part) * chunk
                out_ref[part, :, first : first + chunk] = ref[:, start : start + chunk]


def collect(arrays, parts, blocks, chunk):
    rows = arrays[0].shape[0]
    return pl.pallas_call(
        functools.partial(collect_kernel, parts=parts, blocks=blocks, chunk=chunk),
        out_shape=jax.ShapeDtypeStruct(
            (parts, rows, len(arrays) * blocks * chunk), arrays[0].dtype
        ),
        compiler_params=pltpu.CompilerParams(vmem_limit_bytes=VMEM_LIMIT),
        name="collect",
    )(*arrays)


def spread_kernel(in_ref, *outs, parts, blocks, chunk):
    for number, ref in enumerate(outs):
        for block in range(blocks):
            first = (number * blocks + block) * chunk
            for part in range(parts):
                start = (block * parts + part) * chunk
                ref[:, start : start + chunk] = in_ref[part, :, first : first + chunk].astype(F32)


def spread(array, count, parts, blocks, chunk):
    rows = array.shape[1]
    shape = jax.ShapeDtypeStruct((rows, blocks * parts * chunk), F32)
    return pl.pallas_call(
        functools.partial(spread_kernel, parts=parts, blocks=blocks, chunk=chunk),
        out_shape=[shape] * count,
        compiler_params=pltpu.CompilerParams(vmem_limit_bytes=VMEM_LIMIT),
        name="spread",
    )(array)


def rope_kernel(lin_ref, cos_ref, sin_ref, q_ref, kv_ref, *, heads):
    width = heads * HDIM
    cosine, sine = cos_ref[...], sin_ref[...]
    for part in range(2 * heads):
        columns = slice(part * HDIM, (part + 1) * HDIM)
        value = lin_ref[:, columns].astype(F32)
        turned = (value * cosine + pltpu.roll(value, HDIM // 2, 1) * sine).astype(BF16)
        if part < heads:
            q_ref[:, columns] = turned
        else:
            start = 2 * (part - heads) * HDIM
            kv_ref[:, start : start + HDIM] = turned
            columns = slice((part + heads) * HDIM, (part + heads + 1) * HDIM)
            kv_ref[:, start + HDIM : start + 2 * HDIM] = lin_ref[:, columns]


def rope(linear, cosine, sine, heads, block_rows):
    rows = linear.shape[0]
    width = heads * HDIM
    tile = min(256, block_rows)
    per_block = block_rows // tile
    return pl.pallas_call(
        functools.partial(rope_kernel, heads=heads),
        grid=(rows // tile,),
        in_specs=[
            pl.BlockSpec((tile, 3 * width), lambda i: (i, 0)),
            pl.BlockSpec((tile, HDIM), lambda i: (i % per_block, 0)),
            pl.BlockSpec((tile, HDIM), lambda i: (i % per_block, 0)),
        ],
        out_specs=[
            pl.BlockSpec((tile, width), lambda i: (i, 0)),
            pl.BlockSpec((tile, 2 * width), lambda i: (i, 0)),
        ],
        out_shape=[
            jax.ShapeDtypeStruct((rows, width), BF16),
            jax.ShapeDtypeStruct((rows, 2 * width), BF16),
        ],
        name="rope",
    )(linear, cosine, sine)


def unrope_kernel(place_ref, dq_ref, cos_ref, sin_ref, *refs, heads, masks):
    parts, out_ref = refs[:-1], refs[-1]
    width = heads * HDIM
    me = place_ref[0]
    cosine, sine = cos_ref[...], sin_ref[...]

    def back(value):
        return (value * cosine - pltpu.roll(value, HDIM // 2, 1) * sine).astype(BF16)

    for head in range(heads):
        columns = slice(head * HDIM, (head + 1) * HDIM)
        out_ref[:, columns] = back(dq_ref[:, columns])
    for part in range(2 * heads):
        head, is_value = part // 2, part % 2
        columns = slice(part * HDIM, (part + 1) * HDIM)
        total = parts[0][:, columns].astype(F32)
        for mask, ref in zip(masks[1:], parts[1:]):
            total = total + jnp.where((me ^ mask) > me, ref[:, columns].astype(F32), 0.0)
        start = (1 + is_value) * width + head * HDIM
        out_ref[:, start : start + HDIM] = total.astype(BF16) if is_value else back(total)


def unrope(place, dq, cosine, sine, parts, masks, heads, block_rows):
    rows = dq.shape[0]
    width = heads * HDIM
    tile = min(256, block_rows)
    per_block = block_rows // tile
    return pl.pallas_call(
        functools.partial(unrope_kernel, heads=heads, masks=masks),
        grid_spec=pltpu.PrefetchScalarGridSpec(
            num_scalar_prefetch=1,
            grid=(rows // tile,),
            in_specs=[
                pl.BlockSpec((tile, width), lambda i, *_: (i, 0)),
                pl.BlockSpec((tile, HDIM), lambda i, *_: (i % per_block, 0)),
                pl.BlockSpec((tile, HDIM), lambda i, *_: (i % per_block, 0)),
            ]
            + [pl.BlockSpec((tile, 2 * width), lambda i, *_: (i, 0))] * len(parts),
            out_specs=pl.BlockSpec((tile, 3 * width), lambda i, *_: (i, 0)),
        ),
        out_shape=jax.ShapeDtypeStruct((rows, 3 * width), BF16),
        name="unrope",
    )(place, dq, cosine, sine, *parts)


def visible(first_row, rows, first_key, keys, length):
    row = first_row + lax.broadcasted_iota(jnp.int32, (keys, rows), 1)
    key = first_key + lax.broadcasted_iota(jnp.int32, (keys, rows), 0)
    return (key <= row) & (key < length)

def block_cases(place_ref, mask, block_rows, body):
    me = place_ref[0]
    length = place_ref[1 + pl.program_id(0)]
    if mask == 0:
        body(True, True, me, length)
        return
    source = me ^ mask
    whole = (source + 1) * block_rows <= length
    @pl.when((source < me) & whole)
    def _():
        body(False, False, source, length)
    @pl.when((source < me) & jnp.logical_not(whole))
    def _():
        body(False, True, source, length)

def forward_kernel(place_ref, q_ref, *refs, masks, started, final, tile, block_rows):
    kv_refs, refs = refs[: len(masks)], refs[len(masks) :]
    if started:
        (m_in, l_in, acc_in), refs = refs[:3], refs[3:]
    outs, (m_ref, l_ref, acc_ref) = refs[:-3], refs[-3:]
    if started:
        m_ref[...] = m_in[0]
        l_ref[...] = l_in[0]
        acc_ref[...] = acc_in[0]
    else:
        m_ref[...] = jnp.full(m_ref.shape, NEGATIVE, F32)
        l_ref[...] = jnp.zeros(l_ref.shape, F32)
        acc_ref[...] = jnp.zeros(acc_ref.shape, F32)
    me = place_ref[0]
    for mask, kv_ref in zip(masks, kv_refs):

        def body(diagonal, masked, source, length, kv_ref=kv_ref):
            for first in range(0, block_rows, tile):
                rows = slice(first, first + tile)
                keys = first + tile if diagonal else block_rows
                scores = dot_transposed(kv_ref[:keys, :HDIM], q_ref[rows, :])
                if masked:
                    seen = visible(me * block_rows + first, tile, source * block_rows, keys, length)
                    scores = jnp.where(seen, scores, NEGATIVE)
                peak_old = m_ref[:, rows]
                peak = jnp.maximum(peak_old, jnp.max(scores, axis=0, keepdims=True) * SCALE2)
                shrink = jnp.exp2(peak_old - peak)
                weights = jnp.exp2(scores * SCALE2 - peak)
                l_ref[:, rows] = l_ref[:, rows] * shrink + jnp.sum(weights, axis=0, keepdims=True)
                acc_ref[:, rows] = acc_ref[:, rows] * shrink + outer_sum(
                    kv_ref[:keys, HDIM:], weights.astype(BF16)
                )
                m_ref[:, rows] = peak
        block_cases(place_ref, mask, block_rows, body)
    if final:
        o_ref, lse_ref = outs
        total = l_ref[...]
        o_ref[...] = (acc_ref[...] / total).T.astype(BF16)
        lse_ref[0] = m_ref[...] + jnp.log2(total)
    else:
        for out, ref in zip(outs, (m_ref, l_ref, acc_ref)):
            out[0] = ref[...]

def forward_attention(place, query, blocks, masks, state, final, heads, block_rows):
    rows, width = query.shape
    groups = rows // block_rows * heads
    head_block = pl.BlockSpec((block_rows, HDIM), lambda s, n, *_: (s, n))
    pair_block = pl.BlockSpec((block_rows, 2 * HDIM), lambda s, n, *_: (s, n))
    row_block = pl.BlockSpec((1, 1, block_rows), lambda s, n, *_: (s * heads + n, 0, 0))
    acc_block = pl.BlockSpec((1, HDIM, block_rows), lambda s, n, *_: (s * heads + n, 0, 0))
    row_shape = jax.ShapeDtypeStruct((groups, 1, block_rows), F32)
    acc_shape = jax.ShapeDtypeStruct((groups, HDIM, block_rows), F32)
    if final:
        out_specs, out_shape = [head_block, row_block], [jax.ShapeDtypeStruct((rows, width), BF16), row_shape]
    else:
        out_specs, out_shape = [row_block, row_block, acc_block], [row_shape, row_shape, acc_shape]
    started = state is not None
    operands = [query, *blocks] + (list(state) if started else [])
    return pl.pallas_call(
        functools.partial(forward_kernel, masks=masks, started=started, final=final, tile=min(TILE, block_rows), block_rows=block_rows),
        grid_spec=pltpu.PrefetchScalarGridSpec(
            num_scalar_prefetch=1, grid=(rows // block_rows, heads),
            in_specs=[head_block] + [pair_block] * len(blocks) + ([row_block, row_block, acc_block] if started else []),
            out_specs=out_specs,
            scratch_shapes=[pltpu.VMEM((1, block_rows), F32)] * 2 + [pltpu.VMEM((HDIM, block_rows), F32)],
        ),
        out_shape=out_shape,
        compiler_params=pltpu.CompilerParams(vmem_limit_bytes=VMEM_LIMIT),
        name="attention_forward",
    )(place, *operands)

def backward_kernel(
    place_ref, q_ref, o_ref, do_ref, lse_ref, *refs, masks, started, final, tile, block_rows
):
    kv_refs, refs = refs[: len(masks)], refs[len(masks) :]
    if started:
        dq_in, refs = refs[0], refs[1:]
    dq_ref, dkv_refs, (dq_acc, dk_acc, dv_acc) = refs[0], refs[1:-3], refs[-3:]
    dq_acc[...] = dq_in[0] if started else jnp.zeros(dq_acc.shape, F32)
    me = place_ref[0]
    for mask, kv_ref, dkv_ref in zip(masks, kv_refs, dkv_refs):

        def body(diagonal, masked, source, length, kv_ref=kv_ref, dkv_ref=dkv_ref):
            for first in range(0, block_rows, tile):
                rows = slice(first, first + tile)
                keys = first + tile if diagonal else block_rows
                query, grad = q_ref[rows, :], do_ref[rows, :]
                key, value = kv_ref[:keys, :HDIM], kv_ref[:keys, HDIM:]
                delta = jnp.sum(
                    (grad.astype(F32) * o_ref[rows, :].astype(F32)).T, axis=0, keepdims=True
                )
                scores = dot_transposed(key, query)
                if masked:
                    seen = visible(
                        me * block_rows + first, tile, source * block_rows, keys, length
                    )
                    scores = jnp.where(seen, scores, NEGATIVE)
                probs = jnp.exp2(scores * SCALE2 - lse_ref[0, :, rows])
                prob_grad = dot_transposed(value, grad)
                score_grad = (probs * (prob_grad - delta)).astype(BF16)
                dv = dot(probs.astype(BF16), grad)
                dk = dot(score_grad, query)
                dq_acc[:, rows] += outer_sum(key, score_grad) * SCALE
                if diagonal:
                    if first:
                        dk_acc[:first, :] += dk[:first]
                        dv_acc[:first, :] += dv[:first]
                    dk_acc[rows, :] = dk[first:]
                    dv_acc[rows, :] = dv[first:]
                elif first == 0:
                    dk_acc[...] = dk
                    dv_acc[...] = dv
                else:
                    dk_acc[...] += dk
                    dv_acc[...] += dv
            dkv_ref[:, :HDIM] = (dk_acc[...] * SCALE).astype(BF16)
            dkv_ref[:, HDIM:] = dv_acc[...].astype(BF16)

        block_cases(place_ref, mask, block_rows, body)
    if final:
        dq_ref[...] = dq_acc[...].T
    else:
        dq_ref[0] = dq_acc[...]


def backward_attention(
    place, query, blocks, masks, out, grad, lse, dq, final, heads, block_rows
):
    rows, width = query.shape
    groups = rows // block_rows * heads
    head_block = pl.BlockSpec((block_rows, HDIM), lambda s, n, *_: (s, n))
    pair_block = pl.BlockSpec((block_rows, 2 * HDIM), lambda s, n, *_: (s, n))
    row_block = pl.BlockSpec((1, 1, block_rows), lambda s, n, *_: (s * heads + n, 0, 0))
    acc_block = pl.BlockSpec((1, HDIM, block_rows), lambda s, n, *_: (s * heads + n, 0, 0))
    started = dq is not None
    if final:
        dq_shape = jax.ShapeDtypeStruct((rows, width), F32)
    else:
        dq_shape = jax.ShapeDtypeStruct((groups, HDIM, block_rows), F32)
    dkv_shape = jax.ShapeDtypeStruct((rows, 2 * width), BF16)
    return pl.pallas_call(
        functools.partial(
            backward_kernel,
            masks=masks,
            started=started,
            final=final,
            tile=min(TILE, block_rows),
            block_rows=block_rows,
        ),
        grid_spec=pltpu.PrefetchScalarGridSpec(
            num_scalar_prefetch=1,
            grid=(rows // block_rows, heads),
            in_specs=[head_block] * 3
            + [row_block]
            + [pair_block] * len(masks)
            + ([acc_block] if started else []),
            out_specs=[head_block if final else acc_block] + [pair_block] * len(masks),
            scratch_shapes=[pltpu.VMEM((HDIM, block_rows), F32)]
            + [pltpu.VMEM((block_rows, HDIM), F32)] * 2,
        ),
        out_shape=[dq_shape] + [dkv_shape] * len(masks),
        compiler_params=pltpu.CompilerParams(vmem_limit_bytes=VMEM_LIMIT),
        name="attention_backward",
    )(place, query, out, grad, lse, *blocks, *([dq] if started else []))


def feed_kernel(
    normed_ref, grad_ref, both_ref, down_ref, mixed_ref, back_ref, out_ref, *, columns
):
    hidden = down_ref.shape[0]
    for first in range(0, hidden, columns):
        gates = slice(first, first + columns)
        ups = slice(hidden + first, hidden + first + columns)
        gate_act = dot(normed_ref[...], both_ref[:, gates])
        up_act = dot(normed_ref[...], both_ref[:, ups])
        mixed_grad = dot_transposed(grad_ref[...], down_ref[gates, :])
        sigmoid_gate = 1.0 / (1.0 + jnp.exp(-gate_act))
        silu_gate = gate_act * sigmoid_gate
        mixed_ref[:, gates] = (silu_gate * up_act).astype(BF16)
        slope = sigmoid_gate * (1.0 + gate_act * (1.0 - sigmoid_gate))
        back_ref[:, gates] = (mixed_grad * up_act * slope).astype(BF16)
        back_ref[:, ups] = (mixed_grad * silu_gate).astype(BF16)
    out_ref[...] = dot_transposed(back_ref[...], both_ref[...]).astype(BF16)


def feed_forward(normed, grad, both, down):
    rows, width = normed.shape
    hidden = down.shape[0]
    tile = min(256, rows)

    def by_rows(columns):
        return pl.BlockSpec((tile, columns), lambda i: (i, 0))

    def whole(array):
        return pl.BlockSpec(array.shape, lambda i: (0, 0), pipeline_mode=pl.Buffered(1))

    return pl.pallas_call(
        functools.partial(feed_kernel, columns=min(256, hidden)),
        grid=(rows // tile,),
        in_specs=[by_rows(width), by_rows(width), whole(both), whole(down)],
        out_specs=[by_rows(hidden), by_rows(2 * hidden), by_rows(width)],
        out_shape=[
            jax.ShapeDtypeStruct((rows, hidden), BF16),
            jax.ShapeDtypeStruct((rows, 2 * hidden), BF16),
            jax.ShapeDtypeStruct((rows, width), BF16),
        ],
        compiler_params=pltpu.CompilerParams(vmem_limit_bytes=VMEM_LIMIT),
        name="feed_forward",
    )(normed, grad, both, down)


def local(
    tokens,
    lengths,
    query_weight,
    key_weight,
    value_weight,
    output_weight,
    gate_weight,
    up_weight,
    down_weight,
    cotangent,
):
    blocks = lax.axis_size("blk")
    parts = lax.axis_size("head")
    me = lax.axis_index("blk")
    part = lax.axis_index("head")
    inputs = tokens[0].astype(F32)
    token_count, model_width = inputs.shape
    hidden_width = gate_weight.shape[1]
    heads = HEADS // parts
    width = heads * HDIM
    block_rows = SEQ // blocks
    group_rows = token_count * parts
    slots = group_rows // block_rows
    shard_rows = query_weight.shape[0]
    band_rows = shard_rows * parts
    chunk = hidden_width // (blocks * parts)
    masks = list(range(blocks))
    place = jnp.concatenate([me[None].astype(jnp.int32), lengths.astype(jnp.int32)])

    row_ids = part * token_count + jnp.arange(token_count)
    my_length = jnp.sum(
        jnp.where((row_ids // block_rows)[:, None] == jnp.arange(slots)[None, :], lengths[None, :], 0),
        axis=1,
    )
    valid = (me * block_rows + row_ids % block_rows < my_length).astype(F32)[:, None]

    normed_one, inverse_one = normalize_rows(inputs)
    with jax.named_scope("projection_weights"):
        stacked = collect([query_weight, key_weight, value_weight], parts, 1, width)
        stacked = lax.all_to_all(stacked, "head", split_axis=0, concat_axis=0, tiled=True)
        stacked = stacked.reshape(band_rows, 3 * width)
        normed_start = after(normed_one.astype(BF16), stacked)
        near = send_near(stacked)
        projection = gather_blk(stacked, near + send_far(near)).reshape(model_width, 3 * width)

    with jax.named_scope("tokens_gather"):
        upstream = cotangent[0].astype(F32) * valid
        upstream_low = upstream.astype(BF16)
        normed_group = lax.all_gather(
            normed_start, "head", axis=0, tiled=True
        )

    with jax.named_scope("hidden_weights"):
        both = collect([gate_weight, up_weight], parts, blocks, chunk)
        output_rows = lax.ppermute(
            after(output_weight, stacked),
            ("blk", "head"),
            [(h * blocks + b, b * parts + h) for b in range(blocks) for h in range(parts)],
        )
        output_near = send_near(output_rows)
        output = gather_blk(output_rows, output_near + send_far(output_near))
        output = output.reshape(width, model_width)
        normed_group, projection, output = lax.optimization_barrier(
            (normed_group, projection, output)
        )

    cosine, sine = rotary_tables(me * block_rows + jnp.arange(block_rows))
    with jax.named_scope("projections"):
        linear = dot(normed_group, projection).astype(BF16)
        query, key_value = rope(linear, cosine, sine, heads, block_rows)

    with jax.named_scope("attention"):
        sent = [swapped(key_value, mask, lambda i, j: j > i) for mask in masks[1:]]
        state = forward_attention(
            place, query, [key_value], [0], None, False, heads, block_rows
        )
        both = lax.all_to_all(
            after(both, state[0]), "head", split_axis=0, concat_axis=0, tiled=True
        ).reshape(band_rows, 2 * blocks * chunk)
        upstream_group = lax.all_gather(
            after(upstream_low, normed_group), "head", axis=0, tiled=True
        )
        state, sent, both, upstream_group = lax.optimization_barrier(
            (state, sent, both, upstream_group)
        )
        near = send_near(both)
        attended, log_total = forward_attention(
            place, query, sent, masks[1:], state, True, heads, block_rows
        )
        down_near = send_near(after(down_weight, sent[0]))
        attended, down_near = lax.optimization_barrier((attended, down_near))
        joined = lax.psum_scatter(
            dot(attended, output).astype(BF16), "head", scatter_dimension=0, tiled=True
        )
        joined, near = lax.optimization_barrier((joined, near))
        near, far = lax.optimization_barrier((near, send_far(near)))
        both = gather_blk(both, near + far).reshape(model_width, 2 * blocks * chunk)
        down_near = after(down_near, far)
        down_near, down_far = lax.optimization_barrier((down_near, send_far(down_near)))
        down = gather_blk(down_weight, down_near + down_far).reshape(blocks * chunk, model_width)

    with jax.named_scope("feed_forward"):
        residual = inputs + joined.astype(F32)
        normed_two, inverse_two = normalize_rows(residual)
        normed_two_group = lax.all_gather(normed_two.astype(BF16), "head", axis=0, tiled=True)
        mixed, both_back, normed_two_partial = feed_forward(
            normed_two_group, upstream_group, both, down
        )
        normed_two_grad = lax.psum_scatter(
            normed_two_partial, "head", scatter_dimension=0, tiled=True
        ).astype(F32)
        down_partial = dot(mixed, down).astype(BF16)

        def band(values, place_of):
            return lax.dynamic_slice_in_dim(values, place_of * band_rows, band_rows, 1)

        both_terms = terms_of(lambda j: outer_sum(band(normed_two_group, j), both_back))
        both_passed, both_own = sum_pass(both_terms), sum_own(both_terms)
        down_terms = terms_of(
            lambda j: outer_sum(lax.dynamic_slice_in_dim(mixed, j * chunk, chunk, 1), upstream_group)
        )
        normed_two_grad, down_partial, both_terms, both_passed, both_own, down_terms = (
            lax.optimization_barrier(
                (normed_two_grad, down_partial, both_terms, both_passed, both_own, down_terms)
            )
        )

    residual_grad = upstream + normalize_back(normed_two, inverse_two, normed_two_grad)
    residual_low = residual_grad.astype(BF16)

    def to_shards(summed):
        return lax.all_to_all(
            summed.astype(BF16).reshape(parts, shard_rows, summed.shape[1]),
            "head",
            split_axis=0,
            concat_axis=0,
            tiled=True,
        )

    with jax.named_scope("attention_back"):
        residual_group = lax.all_gather(residual_low, "head", axis=0, tiled=True)
        both_far = sum_far(both_terms, both_passed)
        both_far, down_terms = lax.optimization_barrier((both_far, down_terms))
        both_sum = sum_end(both_terms, both_own, both_far).astype(BF16)
        down_passed, down_own = sum_pass(down_terms), sum_own(down_terms)
        residual_group, both_sum, down_terms, down_passed, down_own = lax.optimization_barrier(
            (residual_group, both_sum, down_terms, down_passed, down_own)
        )
        attended_grad = dot_transposed(residual_group, output).astype(BF16)
        down_act = lax.psum_scatter(
            after(down_partial, residual_group), "head", scatter_dimension=0, tiled=True
        ).astype(F32)
        order = masks[:0:-1] + [0]
        query_grad, *pairs = backward_attention(
            place, query, [([key_value] + sent)[mask] for mask in order], order, attended,
            attended_grad, log_total, None, True, heads, block_rows,
        )
        key_value_grads = [pairs[-1]] + [
            swapped(pairs[order.index(mask)], mask, lambda i, j: j < i) for mask in masks[1:]
        ]
        down_far = sum_far(down_terms, down_passed)
        query_grad, both_sum, down_far = lax.optimization_barrier((query_grad, both_sum, down_far))
        hidden_shards = to_shards(both_sum)
        residual_group = after(residual_group, key_value_grads[1])
        output_terms = terms_of(
            lambda j: outer_sum(
                lax.dynamic_slice_in_dim(attended, j * shard_rows, shard_rows, 1), residual_group
            )
        )
        query_grad, key_value_grads, hidden_shards, output_terms = lax.optimization_barrier(
            (query_grad, key_value_grads, hidden_shards, output_terms)
        )
        down_sum = sum_end(down_terms, down_own, down_far)
        down_act = after(down_act, query_grad)
        layer_output = ((residual + down_act) * valid).astype(BF16)[None]
        projection_back = unrope(
            place, query_grad, cosine, sine, key_value_grads, masks,
            heads, block_rows,
        )
        normed_one_grad = lax.psum_scatter(
            dot_transposed(projection_back, projection).astype(BF16),
            "head",
            scatter_dimension=0,
            tiled=True,
        ).astype(F32)
        tokens_grad = (
            residual_grad + normalize_back(normed_one, inverse_one, normed_one_grad)
        ).astype(BF16)[None]

    with jax.named_scope("weight_grads"):

        gate_grad, up_grad = spread(hidden_shards, 2, parts, blocks, chunk)
        terms = terms_of(lambda j: outer_sum(band(normed_group, j), projection_back))
        summed = sum_end(terms, sum_own(terms), sum_far(terms, sum_pass(terms)))
        summed, output_part = lax.optimization_barrier((summed, sum_to_owner(output_terms)))
        output_grad = lax.ppermute(
            output_part.astype(BF16),
            ("blk", "head"),
            [(b * parts + h, h * blocks + b) for b in range(blocks) for h in range(parts)],
        )
        shards, output_grad, tokens_grad = lax.optimization_barrier(
            (to_shards(summed), output_grad, tokens_grad)
        )
        output_grad = output_grad.astype(F32)
        projection_grads = spread(shards, 3, parts, 1, width)
    return (
        layer_output,
        tokens_grad,
        projection_grads[0],
        projection_grads[1],
        projection_grads[2],
        output_grad,
        gate_grad,
        up_grad,
        down_sum,
    )


def solution(mesh):
    rows = P(("blk", "head"), None)
    places = P("blk", "head", None)
    in_specs = (places, P(), rows, rows, rows, rows, rows, rows, rows, places)
    out_specs = (places, places, rows, rows, rows, rows, rows, rows, rows)
    return jax.shard_map(local, mesh=mesh, in_specs=in_specs, out_specs=out_specs, check_vma=False)
```

```python
import functools
import math

import jax
import jax.numpy as jnp
from jax import lax
from jax.experimental import pallas as pl
from jax.experimental.pallas import tpu as pltpu
from jax.sharding import PartitionSpec as P

HEADS = 16
HDIM = 128
SEQ = 4096

EPSILON = 1e-05
NEGATIVE = -1e30
SCALE = 1.0 / math.sqrt(HDIM)
SCALE2 = SCALE * math.log2(math.e)
TILE = 512
VMEM_LIMIT = 48 * 1024 * 1024
BF16 = jnp.bfloat16
F32 = jnp.float32


def normalize_rows(values):
    centered = values - jnp.mean(values, axis=-1, keepdims=True)
    variance = jnp.mean(centered * centered, axis=-1, keepdims=True)
    inverse = lax.rsqrt(variance + EPSILON)
    return (centered * inverse, inverse)


def normalize_back(normed, inverse, upstream):
    mean_grad = jnp.mean(upstream, axis=-1, keepdims=True)
    mean_proj = jnp.mean(upstream * normed, axis=-1, keepdims=True)
    return inverse * (upstream - mean_grad - normed * mean_proj)


def rotary_tables(positions):
    half_dim = HDIM // 2
    frequency = jnp.exp(
        jnp.arange(half_dim).astype(F32) * (-2.0 * math.log(10000.0) / HDIM)
    )
    angles = positions.astype(F32)[:, None] * frequency[None, :]
    cosine, sine = jnp.cos(angles), jnp.sin(angles)
    return (
        jnp.concatenate([cosine, cosine], axis=1),
        jnp.concatenate([-sine, sine], axis=1),
    )


def dot(left, right):
    return jnp.dot(left, right, preferred_element_type=F32)


def dot_transposed(left, right):
    return lax.dot_general(left, right, (((1,), (1,)), ((), ())), preferred_element_type=F32)


def outer_sum(left, right):
    return lax.dot_general(left, right, (((0,), (0,)), ((), ())), preferred_element_type=F32)


def swapped(value, mask, keep=None):
    peers = lax.axis_size("blk")
    pairs = [(i, i ^ mask) for i in range(peers) if keep is None or keep(i, i ^ mask)]
    return lax.ppermute(value, "blk", pairs)


def after(value, *others):
    return lax.optimization_barrier((value,) + others)[0]


def send_near(value):
    peers = lax.axis_size("blk")
    return [swapped(value, mask) for mask in range(1, 3 if peers == 4 else peers)]


def send_far(near):
    if lax.axis_size("blk") != 4:
        return []
    first, second = near
    half = first.shape[0] // 2
    return [[swapped(first[:half], 2), swapped(second[half:], 1)]]


def gather_blk(value, arrived):
    peers = lax.axis_size("blk")
    me = lax.axis_index("blk")
    whole = jnp.zeros((peers,) + value.shape, value.dtype)
    whole = lax.dynamic_update_index_in_dim(whole, value, me, 0)
    for mask, part in enumerate(arrived, 1):
        row = 0
        for piece in part if isinstance(part, list) else [part]:
            start = (me ^ mask, row) + (0,) * (value.ndim - 1)
            whole = lax.dynamic_update_slice(whole, piece[None], start)
            row += piece.shape[0]
    return whole


def terms_of(part_for):
    peers = lax.axis_size("blk")
    me = lax.axis_index("blk")
    return [part_for(me)] + [part_for(me ^ mask).astype(BF16) for mask in range(1, peers)]


def near_halves(terms):
    half = terms[0].shape[0] // 2
    return ((slice(0, half), 1, 2), (slice(half, None), 2, 1))


def sum_pass(terms):
    if len(terms) != 4:
        return []
    return [swapped(terms[3][rows], near) for rows, near, _ in near_halves(terms)]


def sum_own(terms):
    if len(terms) != 4:
        return [swapped(term, mask) for mask, term in enumerate(terms) if mask]
    return [swapped(terms[near][rows], near) for rows, near, _ in near_halves(terms)]


def sum_far(terms, passed):
    return [
        swapped((terms[far][rows].astype(F32) + part.astype(F32)).astype(BF16), far)
        for part, (rows, _, far) in zip(passed, near_halves(terms))
    ]


def sum_end(terms, own, far):
    total = terms[0]
    if len(terms) != 4:
        for part in own:
            total = total + part.astype(F32)
        return total
    totals = [
        total[rows] + first.astype(F32) + second.astype(F32)
        for first, second, (rows, _, _) in zip(own, far, near_halves(terms))
    ]
    return jnp.concatenate(totals, axis=0)


def sum_to_owner(terms):
    arrived = [swapped(term, mask) for mask, term in enumerate(terms) if mask]
    total = terms[0]
    for part in arrived:
        total = total + part.astype(F32)
    return total


def collect_kernel(*refs, parts, blocks, chunk):
    *ins, out_ref = refs
    for number, ref in enumerate(ins):
        for block in range(blocks):
            first = (number * blocks + block) * chunk
            for part in range(parts):
                start = (block * parts + part) * chunk
                out_ref[part, :, first : first + chunk] = ref[:, start : start + chunk]


def collect(arrays, parts, blocks, chunk):
    rows = arrays[0].shape[0]
    return pl.pallas_call(
        functools.partial(collect_kernel, parts=parts, blocks=blocks, chunk=chunk),
        out_shape=jax.ShapeDtypeStruct(
            (parts, rows, len(arrays) * blocks * chunk), arrays[0].dtype
        ),
        compiler_params=pltpu.CompilerParams(vmem_limit_bytes=VMEM_LIMIT),
        name="collect",
    )(*arrays)


def spread_kernel(in_ref, *outs, parts, blocks, chunk):
    for number, ref in enumerate(outs):
        for block in range(blocks):
            first = (number * blocks + block) * chunk
            for part in range(parts):
                start = (block * parts + part) * chunk
                ref[:, start : start + chunk] = in_ref[part, :, first : first + chunk].astype(F32)


def spread(array, count, parts, blocks, chunk):
    rows = array.shape[1]
    shape = jax.ShapeDtypeStruct((rows, blocks * parts * chunk), F32)
    return pl.pallas_call(
        functools.partial(spread_kernel, parts=parts, blocks=blocks, chunk=chunk),
        out_shape=[shape] * count,
        compiler_params=pltpu.CompilerParams(vmem_limit_bytes=VMEM_LIMIT),
        name="spread",
    )(array)


def project_kernel(normed_ref, weight_ref, cos_ref, sin_ref, q_ref, kv_ref, *, heads):
    cosine, sine = cos_ref[...], sin_ref[...]
    linear = dot(normed_ref[...], weight_ref[...]).astype(BF16)
    for part in range(2 * heads):
        value = linear[:, part * HDIM : (part + 1) * HDIM].astype(F32)
        turned = (value * cosine + pltpu.roll(value, HDIM // 2, 1) * sine).astype(BF16)
        if part < heads:
            q_ref[:, part * HDIM : (part + 1) * HDIM] = turned
        else:
            start = 2 * (part - heads) * HDIM
            kv_ref[:, start : start + HDIM] = turned
            first = (part + heads) * HDIM
            kv_ref[:, start + HDIM : start + 2 * HDIM] = linear[:, first : first + HDIM]


def project(normed, weight, cosine, sine, heads, block_rows):
    rows, model_width = normed.shape
    width = heads * HDIM
    tile = min(256, block_rows)
    per_block = block_rows // tile
    return pl.pallas_call(
        functools.partial(project_kernel, heads=heads),
        grid=(rows // tile,),
        in_specs=[
            pl.BlockSpec((tile, model_width), lambda i: (i, 0)),
            pl.BlockSpec(weight.shape, lambda i: (0, 0), pipeline_mode=pl.Buffered(1)),
            pl.BlockSpec((tile, HDIM), lambda i: (i % per_block, 0)),
            pl.BlockSpec((tile, HDIM), lambda i: (i % per_block, 0)),
        ],
        out_specs=[
            pl.BlockSpec((tile, width), lambda i: (i, 0)),
            pl.BlockSpec((tile, 2 * width), lambda i: (i, 0)),
        ],
        out_shape=[
            jax.ShapeDtypeStruct((rows, width), BF16),
            jax.ShapeDtypeStruct((rows, 2 * width), BF16),
        ],
        compiler_params=pltpu.CompilerParams(vmem_limit_bytes=VMEM_LIMIT),
        name="project",
    )(normed, weight, cosine, sine)


def project_back_kernel(
    place_ref, dq_ref, weight_ref, cos_ref, sin_ref, *refs, heads, masks
):
    parts, out_ref, sum_ref = refs[:-2], refs[-2], refs[-1]
    width = heads * HDIM
    me = place_ref[0]
    cosine, sine = cos_ref[...], sin_ref[...]

    def back(value):
        return (value * cosine - pltpu.roll(value, HDIM // 2, 1) * sine).astype(BF16)

    for head in range(heads):
        columns = slice(head * HDIM, (head + 1) * HDIM)
        out_ref[:, columns] = back(dq_ref[:, columns])
    for part in range(2 * heads):
        head, is_value = part // 2, part % 2
        columns = slice(part * HDIM, (part + 1) * HDIM)
        total = parts[0][:, columns].astype(F32)
        for mask, ref in zip(masks[1:], parts[1:]):
            total = total + jnp.where((me ^ mask) > me, ref[:, columns].astype(F32), 0.0)
        start = (1 + is_value) * width + head * HDIM
        out_ref[:, start : start + HDIM] = total.astype(BF16) if is_value else back(total)
    sum_ref[...] = dot_transposed(out_ref[...], weight_ref[...]).astype(BF16)


def project_back(place, dq, weight, cosine, sine, parts, masks, heads, block_rows):
    rows = dq.shape[0]
    width = heads * HDIM
    model_width = weight.shape[0]
    tile = min(256, block_rows)
    per_block = block_rows // tile
    return pl.pallas_call(
        functools.partial(project_back_kernel, heads=heads, masks=masks),
        grid_spec=pltpu.PrefetchScalarGridSpec(
            num_scalar_prefetch=1,
            grid=(rows // tile,),
            in_specs=[
                pl.BlockSpec((tile, width), lambda i, *_: (i, 0)),
                pl.BlockSpec(weight.shape, lambda i, *_: (0, 0), pipeline_mode=pl.Buffered(1)),
                pl.BlockSpec((tile, HDIM), lambda i, *_: (i % per_block, 0)),
                pl.BlockSpec((tile, HDIM), lambda i, *_: (i % per_block, 0)),
            ]
            + [pl.BlockSpec((tile, 2 * width), lambda i, *_: (i, 0))] * len(parts),
            out_specs=[
                pl.BlockSpec((tile, 3 * width), lambda i, *_: (i, 0)),
                pl.BlockSpec((tile, model_width), lambda i, *_: (i, 0)),
            ],
        ),
        out_shape=[
            jax.ShapeDtypeStruct((rows, 3 * width), BF16),
            jax.ShapeDtypeStruct((rows, model_width), BF16),
        ],
        compiler_params=pltpu.CompilerParams(vmem_limit_bytes=VMEM_LIMIT),
        name="project_back",
    )(place, dq, weight, cosine, sine, *parts)


def norm_kernel(in_ref, part_ref, sum_ref, low_ref):
    total = in_ref[...].astype(F32) + part_ref[...].astype(F32)
    sum_ref[...] = total
    low_ref[...] = normalize_rows(total)[0].astype(BF16)


def add_and_norm(inputs, part):
    rows, width = inputs.shape
    tile = min(64, rows)
    spec = pl.BlockSpec((tile, width), lambda i: (i, 0))
    return pl.pallas_call(
        norm_kernel,
        grid=(rows // tile,),
        in_specs=[spec] * 2,
        out_specs=[spec] * 2,
        out_shape=[
            jax.ShapeDtypeStruct((rows, width), F32),
            jax.ShapeDtypeStruct((rows, width), BF16),
        ],
        compiler_params=pltpu.CompilerParams(vmem_limit_bytes=VMEM_LIMIT),
        name="add_and_norm",
    )(inputs, part)


def norm_back_kernel(in_ref, upstream_ref, grad_ref, *out_refs):
    normed, inverse = normalize_rows(in_ref[...].astype(F32))
    total = upstream_ref[...].astype(F32) + normalize_back(
        normed, inverse, grad_ref[...].astype(F32)
    )
    for ref in out_refs:
        ref[...] = total.astype(ref.dtype)


def norm_back(values, upstream, grad, dtypes):
    rows, width = values.shape
    tile = min(64, rows)
    spec = pl.BlockSpec((tile, width), lambda i: (i, 0))
    return pl.pallas_call(
        norm_back_kernel,
        grid=(rows // tile,),
        in_specs=[spec] * 3,
        out_specs=[spec] * len(dtypes),
        out_shape=[jax.ShapeDtypeStruct((rows, width), dtype) for dtype in dtypes],
        compiler_params=pltpu.CompilerParams(vmem_limit_bytes=VMEM_LIMIT),
        name="norm_back",
    )(values, upstream, grad)


def visible(first_row, rows, first_key, keys, length):
    row = first_row + lax.broadcasted_iota(jnp.int32, (keys, rows), 1)
    key = first_key + lax.broadcasted_iota(jnp.int32, (keys, rows), 0)
    return (key <= row) & (key < length)

def block_cases(place_ref, mask, block_rows, body):
    me = place_ref[0]
    length = place_ref[1 + pl.program_id(0)]
    if mask == 0:
        body(True, True, me, length)
        return
    source = me ^ mask
    whole = (source + 1) * block_rows <= length
    @pl.when((source < me) & whole)
    def _():
        body(False, False, source, length)
    @pl.when((source < me) & jnp.logical_not(whole))
    def _():
        body(False, True, source, length)

def forward_kernel(place_ref, q_ref, *refs, masks, started, final, tile, block_rows):
    kv_refs, refs = refs[: len(masks)], refs[len(masks) :]
    if started:
        (m_in, l_in, acc_in), refs = refs[:3], refs[3:]
    outs, (m_ref, l_ref, acc_ref) = refs[:-3], refs[-3:]
    if started:
        m_ref[...] = m_in[0]
        l_ref[...] = l_in[0]
        acc_ref[...] = acc_in[0]
    else:
        m_ref[...] = jnp.full(m_ref.shape, NEGATIVE, F32)
        l_ref[...] = jnp.zeros(l_ref.shape, F32)
        acc_ref[...] = jnp.zeros(acc_ref.shape, F32)
    me = place_ref[0]
    for mask, kv_ref in zip(masks, kv_refs):

        def body(diagonal, masked, source, length, kv_ref=kv_ref):
            for first in range(0, block_rows, tile):
                rows = slice(first, first + tile)
                keys = first + tile if diagonal else block_rows
                scores = dot_transposed(kv_ref[:keys, :HDIM], q_ref[rows, :])
                if masked:
                    seen = visible(me * block_rows + first, tile, source * block_rows, keys, length)
                    scores = jnp.where(seen, scores, NEGATIVE)
                peak_old = m_ref[:, rows]
                peak = jnp.maximum(peak_old, jnp.max(scores, axis=0, keepdims=True) * SCALE2)
                shrink = jnp.exp2(peak_old - peak)
                weights = jnp.exp2(scores * SCALE2 - peak)
                l_ref[:, rows] = l_ref[:, rows] * shrink + jnp.sum(weights, axis=0, keepdims=True)
                acc_ref[:, rows] = acc_ref[:, rows] * shrink + outer_sum(
                    kv_ref[:keys, HDIM:], weights.astype(BF16)
                )
                m_ref[:, rows] = peak
        block_cases(place_ref, mask, block_rows, body)
    if final:
        o_ref, lse_ref = outs
        total = l_ref[...]
        o_ref[...] = (acc_ref[...] / total).T.astype(BF16)
        lse_ref[0] = m_ref[...] + jnp.log2(total)
    else:
        for out, ref in zip(outs, (m_ref, l_ref, acc_ref)):
            out[0] = ref[...]

def forward_attention(place, query, blocks, masks, state, final, heads, block_rows):
    rows, width = query.shape
    groups = rows // block_rows * heads
    head_block = pl.BlockSpec((block_rows, HDIM), lambda s, n, *_: (s, n))
    pair_block = pl.BlockSpec((block_rows, 2 * HDIM), lambda s, n, *_: (s, n))
    row_block = pl.BlockSpec((1, 1, block_rows), lambda s, n, *_: (s * heads + n, 0, 0))
    acc_block = pl.BlockSpec((1, HDIM, block_rows), lambda s, n, *_: (s * heads + n, 0, 0))
    row_shape = jax.ShapeDtypeStruct((groups, 1, block_rows), F32)
    acc_shape = jax.ShapeDtypeStruct((groups, HDIM, block_rows), F32)
    if final:
        out_specs, out_shape = [head_block, row_block], [jax.ShapeDtypeStruct((rows, width), BF16), row_shape]
    else:
        out_specs, out_shape = [row_block, row_block, acc_block], [row_shape, row_shape, acc_shape]
    started = state is not None
    operands = [query, *blocks] + (list(state) if started else [])
    return pl.pallas_call(
        functools.partial(forward_kernel, masks=masks, started=started, final=final, tile=min(TILE, block_rows), block_rows=block_rows),
        grid_spec=pltpu.PrefetchScalarGridSpec(
            num_scalar_prefetch=1, grid=(rows // block_rows, heads),
            in_specs=[head_block] + [pair_block] * len(blocks) + ([row_block, row_block, acc_block] if started else []),
            out_specs=out_specs,
            scratch_shapes=[pltpu.VMEM((1, block_rows), F32)] * 2 + [pltpu.VMEM((HDIM, block_rows), F32)],
        ),
        out_shape=out_shape,
        compiler_params=pltpu.CompilerParams(vmem_limit_bytes=VMEM_LIMIT),
        name="attention_forward",
    )(place, *operands)

def backward_kernel(
    place_ref, q_ref, o_ref, do_ref, lse_ref, *refs, masks, started, final, tile, block_rows
):
    kv_refs, refs = refs[: len(masks)], refs[len(masks) :]
    if started:
        dq_in, refs = refs[0], refs[1:]
    dq_ref, dkv_refs, (dq_acc, dk_acc, dv_acc) = refs[0], refs[1:-3], refs[-3:]
    dq_acc[...] = dq_in[0] if started else jnp.zeros(dq_acc.shape, F32)
    me = place_ref[0]
    for mask, kv_ref, dkv_ref in zip(masks, kv_refs, dkv_refs):

        def body(diagonal, masked, source, length, kv_ref=kv_ref, dkv_ref=dkv_ref):
            for first in range(0, block_rows, tile):
                rows = slice(first, first + tile)
                keys = first + tile if diagonal else block_rows
                query, grad = q_ref[rows, :], do_ref[rows, :]
                key, value = kv_ref[:keys, :HDIM], kv_ref[:keys, HDIM:]
                delta = jnp.sum(
                    (grad.astype(F32) * o_ref[rows, :].astype(F32)).T, axis=0, keepdims=True
                )
                scores = dot_transposed(key, query)
                if masked:
                    seen = visible(
                        me * block_rows + first, tile, source * block_rows, keys, length
                    )
                    scores = jnp.where(seen, scores, NEGATIVE)
                probs = jnp.exp2(scores * SCALE2 - lse_ref[0, :, rows])
                prob_grad = dot_transposed(value, grad)
                score_grad = (probs * (prob_grad - delta)).astype(BF16)
                dv = dot(probs.astype(BF16), grad)
                dk = dot(score_grad, query)
                dq_acc[:, rows] += outer_sum(key, score_grad) * SCALE
                if diagonal:
                    if first:
                        dk_acc[:first, :] += dk[:first]
                        dv_acc[:first, :] += dv[:first]
                    dk_acc[rows, :] = dk[first:]
                    dv_acc[rows, :] = dv[first:]
                elif first == 0:
                    dk_acc[...] = dk
                    dv_acc[...] = dv
                else:
                    dk_acc[...] += dk
                    dv_acc[...] += dv
            dkv_ref[:, :HDIM] = (dk_acc[...] * SCALE).astype(BF16)
            dkv_ref[:, HDIM:] = dv_acc[...].astype(BF16)

        block_cases(place_ref, mask, block_rows, body)
    if final:
        dq_ref[...] = dq_acc[...].T
    else:
        dq_ref[0] = dq_acc[...]


def backward_attention(
    place, query, blocks, masks, out, grad, lse, dq, final, heads, block_rows
):
    rows, width = query.shape
    groups = rows // block_rows * heads
    head_block = pl.BlockSpec((block_rows, HDIM), lambda s, n, *_: (s, n))
    pair_block = pl.BlockSpec((block_rows, 2 * HDIM), lambda s, n, *_: (s, n))
    row_block = pl.BlockSpec((1, 1, block_rows), lambda s, n, *_: (s * heads + n, 0, 0))
    acc_block = pl.BlockSpec((1, HDIM, block_rows), lambda s, n, *_: (s * heads + n, 0, 0))
    started = dq is not None
    if final:
        dq_shape = jax.ShapeDtypeStruct((rows, width), F32)
    else:
        dq_shape = jax.ShapeDtypeStruct((groups, HDIM, block_rows), F32)
    dkv_shapes = [
        pltpu.HBM((rows, 2 * width), BF16) if mask else jax.ShapeDtypeStruct((rows, 2 * width), BF16)
        for mask in masks
    ]
    return pl.pallas_call(
        functools.partial(
            backward_kernel,
            masks=masks,
            started=started,
            final=final,
            tile=min(TILE, block_rows),
            block_rows=block_rows,
        ),
        grid_spec=pltpu.PrefetchScalarGridSpec(
            num_scalar_prefetch=1,
            grid=(rows // block_rows, heads),
            in_specs=[head_block] * 3
            + [row_block]
            + [pair_block] * len(masks)
            + ([acc_block] if started else []),
            out_specs=[head_block if final else acc_block] + [pair_block] * len(masks),
            scratch_shapes=[pltpu.VMEM((HDIM, block_rows), F32)]
            + [pltpu.VMEM((block_rows, HDIM), F32)] * 2,
        ),
        out_shape=[dq_shape] + dkv_shapes,
        compiler_params=pltpu.CompilerParams(vmem_limit_bytes=VMEM_LIMIT),
        name="attention_backward",
    )(place, query, out, grad, lse, *blocks, *([dq] if started else []))


def feed_kernel(
    normed_ref, grad_ref, both_ref, down_ref, mixed_ref, back_ref, out_ref, *, columns
):
    hidden = down_ref.shape[0]
    for first in range(0, hidden, columns):
        gates = slice(first, first + columns)
        ups = slice(hidden + first, hidden + first + columns)
        gate_act = dot(normed_ref[...], both_ref[:, gates])
        up_act = dot(normed_ref[...], both_ref[:, ups])
        mixed_grad = dot_transposed(grad_ref[...], down_ref[gates, :])
        sigmoid_gate = 1.0 / (1.0 + jnp.exp(-gate_act))
        silu_gate = gate_act * sigmoid_gate
        mixed_ref[:, gates] = (silu_gate * up_act).astype(BF16)
        slope = sigmoid_gate * (1.0 + gate_act * (1.0 - sigmoid_gate))
        back_ref[:, gates] = (mixed_grad * up_act * slope).astype(BF16)
        back_ref[:, ups] = (mixed_grad * silu_gate).astype(BF16)
    out_ref[...] = dot_transposed(back_ref[...], both_ref[...]).astype(BF16)


def feed_forward(normed, grad, both, down):
    rows, width = normed.shape
    hidden = down.shape[0]
    tile = min(256, rows)

    def by_rows(columns):
        return pl.BlockSpec((tile, columns), lambda i: (i, 0))

    def whole(array):
        return pl.BlockSpec(array.shape, lambda i: (0, 0), pipeline_mode=pl.Buffered(1))

    return pl.pallas_call(
        functools.partial(feed_kernel, columns=min(256, hidden)),
        grid=(rows // tile,),
        in_specs=[by_rows(width), by_rows(width), whole(both), whole(down)],
        out_specs=[by_rows(hidden), by_rows(2 * hidden), by_rows(width)],
        out_shape=[
            jax.ShapeDtypeStruct((rows, hidden), BF16),
            jax.ShapeDtypeStruct((rows, 2 * hidden), BF16),
            jax.ShapeDtypeStruct((rows, width), BF16),
        ],
        compiler_params=pltpu.CompilerParams(vmem_limit_bytes=VMEM_LIMIT),
        name="feed_forward",
    )(normed, grad, both, down)


def local(
    tokens,
    lengths,
    query_weight,
    key_weight,
    value_weight,
    output_weight,
    gate_weight,
    up_weight,
    down_weight,
    cotangent,
):
    blocks = lax.axis_size("blk")
    parts = lax.axis_size("head")
    me = lax.axis_index("blk")
    part = lax.axis_index("head")
    inputs = tokens[0].astype(F32)
    token_count, model_width = inputs.shape
    hidden_width = gate_weight.shape[1]
    heads = HEADS // parts
    width = heads * HDIM
    block_rows = SEQ // blocks
    group_rows = token_count * parts
    slots = group_rows // block_rows
    shard_rows = query_weight.shape[0]
    band_rows = shard_rows * parts
    chunk = hidden_width // (blocks * parts)
    masks = list(range(blocks))
    place = jnp.concatenate([me[None].astype(jnp.int32), lengths.astype(jnp.int32)])

    row_ids = part * token_count + jnp.arange(token_count)
    my_length = jnp.sum(
        jnp.where((row_ids // block_rows)[:, None] == jnp.arange(slots)[None, :], lengths[None, :], 0),
        axis=1,
    )
    valid = (me * block_rows + row_ids % block_rows < my_length).astype(F32)[:, None]

    normed_one = normalize_rows(inputs)[0]
    with jax.named_scope("projection_weights"):
        stacked = collect([query_weight, key_weight, value_weight], parts, 1, width)
        stacked = lax.all_to_all(stacked, "head", split_axis=0, concat_axis=0, tiled=True)
        stacked = stacked.reshape(band_rows, 3 * width)
        normed_start = after(normed_one.astype(BF16), stacked)
        near = send_near(stacked)
        far = send_far(near)
        projection = gather_blk(stacked, near + far).reshape(model_width, 3 * width)

    with jax.named_scope("tokens_gather"):
        upstream_low = (cotangent[0].astype(F32) * valid).astype(BF16)
        normed_group = lax.all_gather(
            normed_start, "head", axis=0, tiled=True
        )

    with jax.named_scope("hidden_weights"):
        both = collect([gate_weight, up_weight], parts, blocks, chunk)
        output_rows = lax.ppermute(
            after(output_weight, stacked),
            ("blk", "head"),
            [(h * blocks + b, b * parts + h) for b in range(blocks) for h in range(parts)],
        )
        output_rows = after(output_rows, far)
        output_near = send_near(output_rows)
        output = gather_blk(output_rows, output_near + send_far(output_near))
        output = output.reshape(width, model_width)
        normed_group, projection, output = lax.optimization_barrier(
            (normed_group, projection, output)
        )

    cosine, sine = rotary_tables(me * block_rows + jnp.arange(block_rows))
    with jax.named_scope("projections"):
        query, key_value = project(normed_group, projection, cosine, sine, heads, block_rows)

    with jax.named_scope("attention"):
        sent = [swapped(key_value, mask, lambda i, j: j > i) for mask in masks[1:]]
        upstream_group = lax.all_gather(
            after(upstream_low, normed_group), "head", axis=0, tiled=True
        )
        both = lax.all_to_all(
            after(both, upstream_group, *sent), "head", split_axis=0, concat_axis=0, tiled=True
        ).reshape(band_rows, 2 * blocks * chunk)
        attended, log_total = forward_attention(
            place, query, [key_value] + sent, masks, None, True, heads, block_rows
        )
        down_near = send_near(after(down_weight, sent[0]))
        joined_partial = dot(after(attended, down_near), output).astype(BF16)
        joined_partial, down_near, both = lax.optimization_barrier(
            (joined_partial, down_near, both)
        )
        near = send_near(both)
        joined = lax.psum_scatter(joined_partial, "head", scatter_dimension=0, tiled=True)
        joined, near = lax.optimization_barrier((joined, near))
        near, far = lax.optimization_barrier((near, send_far(near)))
        both = gather_blk(both, near + far).reshape(model_width, 2 * blocks * chunk)
        down_near = after(down_near, far)
        down_near, down_far = lax.optimization_barrier((down_near, send_far(down_near)))
        down = gather_blk(down_weight, down_near + down_far).reshape(blocks * chunk, model_width)

    with jax.named_scope("feed_forward"):
        residual, normed_two = add_and_norm(tokens[0], joined)
        normed_two_group = lax.all_gather(normed_two, "head", axis=0, tiled=True)
        mixed, both_back, normed_two_partial = feed_forward(
            normed_two_group, upstream_group, both, down
        )
        normed_two_grad = lax.psum_scatter(
            normed_two_partial, "head", scatter_dimension=0, tiled=True
        )
        down_partial = dot(mixed, down).astype(BF16)

        def band(values, place_of):
            return lax.dynamic_slice_in_dim(values, place_of * band_rows, band_rows, 1)

        both_terms = terms_of(lambda j: outer_sum(band(normed_two_group, j), both_back))
        both_passed = sum_pass(both_terms)
        down_terms = terms_of(
            lambda j: outer_sum(lax.dynamic_slice_in_dim(mixed, j * chunk, chunk, 1), upstream_group)
        )
        normed_two_grad, down_partial, both_terms, both_passed, down_terms = (
            lax.optimization_barrier(
                (normed_two_grad, down_partial, both_terms, both_passed, down_terms)
            )
        )

    residual_grad, residual_low = norm_back(residual, upstream_low, normed_two_grad, (F32, BF16))

    def to_shards(summed):
        return lax.all_to_all(
            summed.astype(BF16).reshape(parts, shard_rows, summed.shape[1]),
            "head",
            split_axis=0,
            concat_axis=0,
            tiled=True,
        )

    with jax.named_scope("attention_back"):
        residual_group = lax.all_gather(residual_low, "head", axis=0, tiled=True)
        both_own, both_far = sum_own(both_terms), sum_far(both_terms, both_passed)
        both_sum = sum_end(both_terms, both_own, both_far).astype(BF16)
        residual_group, both_sum, down_terms = lax.optimization_barrier(
            (residual_group, both_sum, down_terms)
        )
        down_passed, down_own = sum_pass(down_terms), sum_own(down_terms)
        attended_grad = dot_transposed(residual_group, output).astype(BF16)
        down_act = lax.psum_scatter(
            after(down_partial, residual_group), "head", scatter_dimension=0, tiled=True
        ).astype(F32)
        order = masks[:0:-1] + [0]
        query_grad, *pairs = backward_attention(
            place, query, [([key_value] + sent)[mask] for mask in order], order, attended,
            attended_grad, log_total, None, True, heads, block_rows,
        )
        key_value_grads = [pairs[-1]] + [
            swapped(pairs[order.index(mask)], mask, lambda i, j: j < i) for mask in masks[1:]
        ]
        query_grad, both_sum, down_passed, down_own = lax.optimization_barrier(
            (query_grad, both_sum, down_passed, down_own)
        )
        hidden_shards = to_shards(both_sum)
        residual_group = after(residual_group, key_value_grads[1])
        output_terms = terms_of(
            lambda j: outer_sum(
                lax.dynamic_slice_in_dim(attended, j * shard_rows, shard_rows, 1), residual_group
            )
        )
        query_grad, key_value_grads, hidden_shards, output_terms = lax.optimization_barrier(
            (query_grad, key_value_grads, hidden_shards, output_terms)
        )
        down_act = after(down_act, query_grad)
        layer_output = ((residual + down_act) * valid).astype(BF16)[None]
        projection_back, normed_one_partial = project_back(
            place, query_grad, projection, cosine, sine, key_value_grads, masks,
            heads, block_rows,
        )
        normed_one_grad = lax.psum_scatter(
            normed_one_partial, "head", scatter_dimension=0, tiled=True
        )
        (tokens_grad,) = norm_back(tokens[0], residual_grad, normed_one_grad, (BF16,))
        tokens_grad = tokens_grad[None]

    with jax.named_scope("weight_grads"):

        gate_grad, up_grad = spread(hidden_shards, 2, parts, blocks, chunk)
        terms = terms_of(lambda j: outer_sum(band(normed_group, j), projection_back))
        passed, own = sum_pass(terms), sum_own(terms)
        passed, own, terms, output_terms, gate_grad, up_grad = lax.optimization_barrier(
            (passed, own, terms, output_terms, gate_grad, up_grad)
        )
        summed = sum_end(terms, own, sum_far(terms, passed))
        summed, output_part, down_passed = lax.optimization_barrier(
            (summed, sum_to_owner(output_terms), down_passed)
        )
        down_sum = sum_end(down_terms, down_own, sum_far(down_terms, down_passed))
        output_grad = lax.ppermute(
            output_part.astype(BF16),
            ("blk", "head"),
            [(b * parts + h, h * blocks + b) for b in range(blocks) for h in range(parts)],
        )
        shards, output_grad, tokens_grad = lax.optimization_barrier(
            (to_shards(summed), output_grad, tokens_grad)
        )
        output_grad = output_grad.astype(F32)
        projection_grads = spread(shards, 3, parts, 1, width)
    return (
        layer_output,
        tokens_grad,
        projection_grads[0],
        projection_grads[1],
        projection_grads[2],
        output_grad,
        gate_grad,
        up_grad,
        down_sum,
    )


def solution(mesh):
    rows = P(("blk", "head"), None)
    places = P("blk", "head", None)
    in_specs = (places, P(), rows, rows, rows, rows, rows, rows, rows, places)
    out_specs = (places, places, rows, rows, rows, rows, rows, rows, rows)
    return jax.shard_map(local, mesh=mesh, in_specs=in_specs, out_specs=out_specs, check_vma=False)
```

```python
import functools
import math

import jax
import jax.numpy as jnp
from jax import lax
from jax.experimental import pallas as pl
from jax.experimental.pallas import tpu as pltpu
from jax.sharding import PartitionSpec as P

HEADS = 16
HDIM = 128
SEQ = 4096

EPSILON = 1e-05
NEGATIVE = -1e30
SCALE = 1.0 / math.sqrt(HDIM)
SCALE2 = SCALE * math.log2(math.e)
TILE = 512
VMEM_LIMIT = 48 * 1024 * 1024
BF16 = jnp.bfloat16
F32 = jnp.float32


def normalize_rows(values):
    centered = values - jnp.mean(values, axis=-1, keepdims=True)
    variance = jnp.mean(centered * centered, axis=-1, keepdims=True)
    inverse = lax.rsqrt(variance + EPSILON)
    return (centered * inverse, inverse)


def normalize_back(normed, inverse, upstream):
    mean_grad = jnp.mean(upstream, axis=-1, keepdims=True)
    mean_proj = jnp.mean(upstream * normed, axis=-1, keepdims=True)
    return inverse * (upstream - mean_grad - normed * mean_proj)


def rotary_tables(positions):
    half_dim = HDIM // 2
    frequency = jnp.exp(
        jnp.arange(half_dim).astype(F32) * (-2.0 * math.log(10000.0) / HDIM)
    )
    angles = positions.astype(F32)[:, None] * frequency[None, :]
    cosine, sine = jnp.cos(angles), jnp.sin(angles)
    return (
        jnp.concatenate([cosine, cosine], axis=1),
        jnp.concatenate([-sine, sine], axis=1),
    )


def dot(left, right):
    return jnp.dot(left, right, preferred_element_type=F32)


def dot_transposed(left, right):
    return lax.dot_general(left, right, (((1,), (1,)), ((), ())), preferred_element_type=F32)


def outer_sum(left, right):
    return lax.dot_general(left, right, (((0,), (0,)), ((), ())), preferred_element_type=F32)


def swapped(value, mask, keep=None):
    peers = lax.axis_size("blk")
    pairs = [(i, i ^ mask) for i in range(peers) if keep is None or keep(i, i ^ mask)]
    return lax.ppermute(value, "blk", pairs)


def after(value, *others):
    return lax.optimization_barrier((value,) + others)[0]


def send_near(value):
    peers = lax.axis_size("blk")
    return [swapped(value, mask) for mask in range(1, 3 if peers == 4 else peers)]


def send_far(near):
    if lax.axis_size("blk") != 4:
        return []
    first, second = near
    half = first.shape[0] // 2
    return [[swapped(first[:half], 2), swapped(second[half:], 1)]]


def gather_blk(value, arrived):
    peers = lax.axis_size("blk")
    me = lax.axis_index("blk")
    whole = jnp.zeros((peers,) + value.shape, value.dtype)
    whole = lax.dynamic_update_index_in_dim(whole, value, me, 0)
    for mask, part in enumerate(arrived, 1):
        row = 0
        for piece in part if isinstance(part, list) else [part]:
            start = (me ^ mask, row) + (0,) * (value.ndim - 1)
            whole = lax.dynamic_update_slice(whole, piece[None], start)
            row += piece.shape[0]
    return whole


def terms_of(part_for):
    peers = lax.axis_size("blk")
    me = lax.axis_index("blk")
    return [part_for(me)] + [part_for(me ^ mask).astype(BF16) for mask in range(1, peers)]


def near_halves(terms):
    half = terms[0].shape[0] // 2
    return ((slice(0, half), 1, 2), (slice(half, None), 2, 1))


def sum_pass(terms):
    if len(terms) != 4:
        return []
    return [swapped(terms[3][rows], near) for rows, near, _ in near_halves(terms)]


def sum_own(terms):
    if len(terms) != 4:
        return [swapped(term, mask) for mask, term in enumerate(terms) if mask]
    return [swapped(terms[near][rows], near) for rows, near, _ in near_halves(terms)]


def sum_far(terms, passed):
    return [
        swapped((terms[far][rows].astype(F32) + part.astype(F32)).astype(BF16), far)
        for part, (rows, _, far) in zip(passed, near_halves(terms))
    ]


def sum_end(terms, own, far):
    total = terms[0]
    if len(terms) != 4:
        for part in own:
            total = total + part.astype(F32)
        return total
    totals = [
        total[rows] + first.astype(F32) + second.astype(F32)
        for first, second, (rows, _, _) in zip(own, far, near_halves(terms))
    ]
    return jnp.concatenate(totals, axis=0)


def sum_to_owner(terms):
    arrived = [swapped(term, mask) for mask, term in enumerate(terms) if mask]
    total = terms[0]
    for part in arrived:
        total = total + part.astype(F32)
    return total


def collect_kernel(*refs, parts, blocks, chunk):
    *ins, out_ref = refs
    for number, ref in enumerate(ins):
        for block in range(blocks):
            first = (number * blocks + block) * chunk
            for part in range(parts):
                start = (block * parts + part) * chunk
                out_ref[part, :, first : first + chunk] = ref[:, start : start + chunk]


def collect(arrays, parts, blocks, chunk):
    rows = arrays[0].shape[0]
    return pl.pallas_call(
        functools.partial(collect_kernel, parts=parts, blocks=blocks, chunk=chunk),
        out_shape=jax.ShapeDtypeStruct(
            (parts, rows, len(arrays) * blocks * chunk), arrays[0].dtype
        ),
        compiler_params=pltpu.CompilerParams(vmem_limit_bytes=VMEM_LIMIT),
        name="collect",
    )(*arrays)


def spread_kernel(in_ref, *outs, parts, blocks, chunk):
    for number, ref in enumerate(outs):
        for block in range(blocks):
            first = (number * blocks + block) * chunk
            for part in range(parts):
                start = (block * parts + part) * chunk
                ref[:, start : start + chunk] = in_ref[part, :, first : first + chunk].astype(F32)


def spread(array, count, parts, blocks, chunk):
    rows = array.shape[1]
    shape = jax.ShapeDtypeStruct((rows, blocks * parts * chunk), F32)
    return pl.pallas_call(
        functools.partial(spread_kernel, parts=parts, blocks=blocks, chunk=chunk),
        out_shape=[shape] * count,
        compiler_params=pltpu.CompilerParams(vmem_limit_bytes=VMEM_LIMIT),
        name="spread",
    )(array)


def project_kernel(normed_ref, weight_ref, cos_ref, sin_ref, q_ref, kv_ref, *, heads):
    cosine, sine = cos_ref[...], sin_ref[...]
    linear = dot(normed_ref[...], weight_ref[...]).astype(BF16)
    for part in range(2 * heads):
        value = linear[:, part * HDIM : (part + 1) * HDIM].astype(F32)
        turned = (value * cosine + pltpu.roll(value, HDIM // 2, 1) * sine).astype(BF16)
        if part < heads:
            q_ref[:, part * HDIM : (part + 1) * HDIM] = turned
        else:
            start = 2 * (part - heads) * HDIM
            kv_ref[:, start : start + HDIM] = turned
            first = (part + heads) * HDIM
            kv_ref[:, start + HDIM : start + 2 * HDIM] = linear[:, first : first + HDIM]


def project(normed, weight, cosine, sine, heads, block_rows):
    rows, model_width = normed.shape
    width = heads * HDIM
    tile = min(256, block_rows)
    per_block = block_rows // tile
    return pl.pallas_call(
        functools.partial(project_kernel, heads=heads),
        grid=(rows // tile,),
        in_specs=[
            pl.BlockSpec((tile, model_width), lambda i: (i, 0)),
            pl.BlockSpec(weight.shape, lambda i: (0, 0), pipeline_mode=pl.Buffered(1)),
            pl.BlockSpec((tile, HDIM), lambda i: (i % per_block, 0)),
            pl.BlockSpec((tile, HDIM), lambda i: (i % per_block, 0)),
        ],
        out_specs=[
            pl.BlockSpec((tile, width), lambda i: (i, 0)),
            pl.BlockSpec((tile, 2 * width), lambda i: (i, 0)),
        ],
        out_shape=[
            jax.ShapeDtypeStruct((rows, width), BF16),
            jax.ShapeDtypeStruct((rows, 2 * width), BF16),
        ],
        compiler_params=pltpu.CompilerParams(vmem_limit_bytes=VMEM_LIMIT),
        name="project",
    )(normed, weight, cosine, sine)


def project_back_kernel(
    place_ref, dq_ref, weight_ref, cos_ref, sin_ref, *refs, heads, masks
):
    parts, out_ref, sum_ref = refs[:-2], refs[-2], refs[-1]
    width = heads * HDIM
    me = place_ref[0]
    cosine, sine = cos_ref[...], sin_ref[...]

    def back(value):
        return (value * cosine - pltpu.roll(value, HDIM // 2, 1) * sine).astype(BF16)

    for head in range(heads):
        columns = slice(head * HDIM, (head + 1) * HDIM)
        out_ref[:, columns] = back(dq_ref[:, columns])
    for part in range(2 * heads):
        head, is_value = part // 2, part % 2
        columns = slice(part * HDIM, (part + 1) * HDIM)
        total = parts[0][:, columns].astype(F32)
        for mask, ref in zip(masks[1:], parts[1:]):
            total = total + jnp.where((me ^ mask) > me, ref[:, columns].astype(F32), 0.0)
        start = (1 + is_value) * width + head * HDIM
        out_ref[:, start : start + HDIM] = total.astype(BF16) if is_value else back(total)
    sum_ref[...] = dot_transposed(out_ref[...], weight_ref[...]).astype(BF16)


def project_back(place, dq, weight, cosine, sine, parts, masks, heads, block_rows):
    rows = dq.shape[0]
    width = heads * HDIM
    model_width = weight.shape[0]
    tile = min(256, block_rows)
    per_block = block_rows // tile
    return pl.pallas_call(
        functools.partial(project_back_kernel, heads=heads, masks=masks),
        grid_spec=pltpu.PrefetchScalarGridSpec(
            num_scalar_prefetch=1,
            grid=(rows // tile,),
            in_specs=[
                pl.BlockSpec((tile, width), lambda i, *_: (i, 0)),
                pl.BlockSpec(weight.shape, lambda i, *_: (0, 0), pipeline_mode=pl.Buffered(1)),
                pl.BlockSpec((tile, HDIM), lambda i, *_: (i % per_block, 0)),
                pl.BlockSpec((tile, HDIM), lambda i, *_: (i % per_block, 0)),
            ]
            + [pl.BlockSpec((tile, 2 * width), lambda i, *_: (i, 0))] * len(parts),
            out_specs=[
                pl.BlockSpec((tile, 3 * width), lambda i, *_: (i, 0)),
                pl.BlockSpec((tile, model_width), lambda i, *_: (i, 0)),
            ],
        ),
        out_shape=[
            jax.ShapeDtypeStruct((rows, 3 * width), BF16),
            jax.ShapeDtypeStruct((rows, model_width), BF16),
        ],
        compiler_params=pltpu.CompilerParams(vmem_limit_bytes=VMEM_LIMIT),
        name="project_back",
    )(place, dq, weight, cosine, sine, *parts)


def norm_kernel(in_ref, part_ref, sum_ref, low_ref):
    total = in_ref[...].astype(F32) + part_ref[...].astype(F32)
    sum_ref[...] = total
    low_ref[...] = normalize_rows(total)[0].astype(BF16)


def add_and_norm(inputs, part):
    rows, width = inputs.shape
    tile = min(64, rows)
    spec = pl.BlockSpec((tile, width), lambda i: (i, 0))
    return pl.pallas_call(
        norm_kernel,
        grid=(rows // tile,),
        in_specs=[spec] * 2,
        out_specs=[spec] * 2,
        out_shape=[
            jax.ShapeDtypeStruct((rows, width), F32),
            jax.ShapeDtypeStruct((rows, width), BF16),
        ],
        compiler_params=pltpu.CompilerParams(vmem_limit_bytes=VMEM_LIMIT),
        name="add_and_norm",
    )(inputs, part)


def norm_back_kernel(in_ref, upstream_ref, grad_ref, *out_refs):
    normed, inverse = normalize_rows(in_ref[...].astype(F32))
    total = upstream_ref[...].astype(F32) + normalize_back(
        normed, inverse, grad_ref[...].astype(F32)
    )
    for ref in out_refs:
        ref[...] = total.astype(ref.dtype)


def norm_back(values, upstream, grad, dtypes):
    rows, width = values.shape
    tile = min(64, rows)
    spec = pl.BlockSpec((tile, width), lambda i: (i, 0))
    return pl.pallas_call(
        norm_back_kernel,
        grid=(rows // tile,),
        in_specs=[spec] * 3,
        out_specs=[spec] * len(dtypes),
        out_shape=[jax.ShapeDtypeStruct((rows, width), dtype) for dtype in dtypes],
        compiler_params=pltpu.CompilerParams(vmem_limit_bytes=VMEM_LIMIT),
        name="norm_back",
    )(values, upstream, grad)


def visible(first_row, rows, first_key, keys, length):
    row = first_row + lax.broadcasted_iota(jnp.int32, (keys, rows), 1)
    key = first_key + lax.broadcasted_iota(jnp.int32, (keys, rows), 0)
    return (key <= row) & (key < length)

def block_cases(place_ref, mask, block_rows, body):
    me = place_ref[0]
    length = place_ref[1 + pl.program_id(0)]
    if mask == 0:
        body(True, True, me, length)
        return
    source = me ^ mask
    whole = (source + 1) * block_rows <= length
    @pl.when((source < me) & whole)
    def _():
        body(False, False, source, length)
    @pl.when((source < me) & jnp.logical_not(whole))
    def _():
        body(False, True, source, length)

def forward_kernel(place_ref, q_ref, *refs, masks, started, final, tile, block_rows):
    kv_refs, refs = refs[: len(masks)], refs[len(masks) :]
    if started:
        (m_in, l_in, acc_in), refs = refs[:3], refs[3:]
    outs, (m_ref, l_ref, acc_ref) = refs[:-3], refs[-3:]
    if started:
        m_ref[...] = m_in[0]
        l_ref[...] = l_in[0]
        acc_ref[...] = acc_in[0]
    else:
        m_ref[...] = jnp.full(m_ref.shape, NEGATIVE, F32)
        l_ref[...] = jnp.zeros(l_ref.shape, F32)
        acc_ref[...] = jnp.zeros(acc_ref.shape, F32)
    me = place_ref[0]
    for mask, kv_ref in zip(masks, kv_refs):

        def body(diagonal, masked, source, length, kv_ref=kv_ref):
            for first in range(0, block_rows, tile):
                rows = slice(first, first + tile)
                keys = first + tile if diagonal else block_rows
                scores = dot_transposed(kv_ref[:keys, :HDIM], q_ref[rows, :])
                if masked:
                    seen = visible(me * block_rows + first, tile, source * block_rows, keys, length)
                    scores = jnp.where(seen, scores, NEGATIVE)
                peak_old = m_ref[:, rows]
                peak = jnp.maximum(peak_old, jnp.max(scores, axis=0, keepdims=True) * SCALE2)
                shrink = jnp.exp2(peak_old - peak)
                weights = jnp.exp2(scores * SCALE2 - peak)
                l_ref[:, rows] = l_ref[:, rows] * shrink + jnp.sum(weights, axis=0, keepdims=True)
                acc_ref[:, rows] = acc_ref[:, rows] * shrink + outer_sum(
                    kv_ref[:keys, HDIM:], weights.astype(BF16)
                )
                m_ref[:, rows] = peak
        block_cases(place_ref, mask, block_rows, body)
    if final:
        o_ref, lse_ref = outs
        total = l_ref[...]
        o_ref[...] = (acc_ref[...] / total).T.astype(BF16)
        lse_ref[0] = m_ref[...] + jnp.log2(total)
    else:
        for out, ref in zip(outs, (m_ref, l_ref, acc_ref)):
            out[0] = ref[...]

def forward_attention(place, query, blocks, masks, state, final, heads, block_rows):
    rows, width = query.shape
    groups = rows // block_rows * heads
    head_block = pl.BlockSpec((block_rows, HDIM), lambda s, n, *_: (s, n))
    pair_block = pl.BlockSpec((block_rows, 2 * HDIM), lambda s, n, *_: (s, n))
    row_block = pl.BlockSpec((1, 1, block_rows), lambda s, n, *_: (s * heads + n, 0, 0))
    acc_block = pl.BlockSpec((1, HDIM, block_rows), lambda s, n, *_: (s * heads + n, 0, 0))
    row_shape = jax.ShapeDtypeStruct((groups, 1, block_rows), F32)
    acc_shape = jax.ShapeDtypeStruct((groups, HDIM, block_rows), F32)
    if final:
        out_specs, out_shape = [head_block, row_block], [jax.ShapeDtypeStruct((rows, width), BF16), row_shape]
    else:
        out_specs, out_shape = [row_block, row_block, acc_block], [row_shape, row_shape, acc_shape]
    started = state is not None
    operands = [query, *blocks] + (list(state) if started else [])
    return pl.pallas_call(
        functools.partial(forward_kernel, masks=masks, started=started, final=final, tile=min(TILE, block_rows), block_rows=block_rows),
        grid_spec=pltpu.PrefetchScalarGridSpec(
            num_scalar_prefetch=1, grid=(rows // block_rows, heads),
            in_specs=[head_block] + [pair_block] * len(blocks) + ([row_block, row_block, acc_block] if started else []),
            out_specs=out_specs,
            scratch_shapes=[pltpu.VMEM((1, block_rows), F32)] * 2 + [pltpu.VMEM((HDIM, block_rows), F32)],
        ),
        out_shape=out_shape,
        compiler_params=pltpu.CompilerParams(vmem_limit_bytes=VMEM_LIMIT),
        name="attention_forward",
    )(place, *operands)

def backward_kernel(
    place_ref, q_ref, o_ref, do_ref, lse_ref, *refs, masks, started, final, tile, block_rows
):
    kv_refs, refs = refs[: len(masks)], refs[len(masks) :]
    if started:
        dq_in, refs = refs[0], refs[1:]
    dq_ref, dkv_refs, (dq_acc, dk_acc, dv_acc) = refs[0], refs[1:-3], refs[-3:]
    dq_acc[...] = dq_in[0] if started else jnp.zeros(dq_acc.shape, F32)
    me = place_ref[0]
    for mask, kv_ref, dkv_ref in zip(masks, kv_refs, dkv_refs):

        def body(diagonal, masked, source, length, kv_ref=kv_ref, dkv_ref=dkv_ref):
            for first in range(0, block_rows, tile):
                rows = slice(first, first + tile)
                keys = first + tile if diagonal else block_rows
                query, grad = q_ref[rows, :], do_ref[rows, :]
                key, value = kv_ref[:keys, :HDIM], kv_ref[:keys, HDIM:]
                delta = jnp.sum(
                    (grad.astype(F32) * o_ref[rows, :].astype(F32)).T, axis=0, keepdims=True
                )
                scores = dot_transposed(key, query)
                if masked:
                    seen = visible(
                        me * block_rows + first, tile, source * block_rows, keys, length
                    )
                    scores = jnp.where(seen, scores, NEGATIVE)
                probs = jnp.exp2(scores * SCALE2 - lse_ref[0, :, rows])
                prob_grad = dot_transposed(value, grad)
                score_grad = (probs * (prob_grad - delta)).astype(BF16)
                dv = dot(probs.astype(BF16), grad)
                dk = dot(score_grad, query)
                dq_acc[:, rows] += outer_sum(key, score_grad) * SCALE
                if diagonal:
                    if first:
                        dk_acc[:first, :] += dk[:first]
                        dv_acc[:first, :] += dv[:first]
                    dk_acc[rows, :] = dk[first:]
                    dv_acc[rows, :] = dv[first:]
                elif first == 0:
                    dk_acc[...] = dk
                    dv_acc[...] = dv
                else:
                    dk_acc[...] += dk
                    dv_acc[...] += dv
            dkv_ref[:, :HDIM] = (dk_acc[...] * SCALE).astype(BF16)
            dkv_ref[:, HDIM:] = dv_acc[...].astype(BF16)

        block_cases(place_ref, mask, block_rows, body)
    if final:
        dq_ref[...] = dq_acc[...].T
    else:
        dq_ref[0] = dq_acc[...]


def backward_attention(
    place, query, blocks, masks, out, grad, lse, dq, final, heads, block_rows
):
    rows, width = query.shape
    groups = rows // block_rows * heads
    head_block = pl.BlockSpec((block_rows, HDIM), lambda s, n, *_: (s, n))
    pair_block = pl.BlockSpec((block_rows, 2 * HDIM), lambda s, n, *_: (s, n))
    row_block = pl.BlockSpec((1, 1, block_rows), lambda s, n, *_: (s * heads + n, 0, 0))
    acc_block = pl.BlockSpec((1, HDIM, block_rows), lambda s, n, *_: (s * heads + n, 0, 0))
    started = dq is not None
    if final:
        dq_shape = jax.ShapeDtypeStruct((rows, width), F32)
    else:
        dq_shape = jax.ShapeDtypeStruct((groups, HDIM, block_rows), F32)
    dkv_shapes = [
        pltpu.HBM((rows, 2 * width), BF16) if mask else jax.ShapeDtypeStruct((rows, 2 * width), BF16)
        for mask in masks
    ]
    return pl.pallas_call(
        functools.partial(
            backward_kernel,
            masks=masks,
            started=started,
            final=final,
            tile=min(TILE, block_rows),
            block_rows=block_rows,
        ),
        grid_spec=pltpu.PrefetchScalarGridSpec(
            num_scalar_prefetch=1,
            grid=(rows // block_rows, heads),
            in_specs=[head_block] * 3
            + [row_block]
            + [pair_block] * len(masks)
            + ([acc_block] if started else []),
            out_specs=[head_block if final else acc_block] + [pair_block] * len(masks),
            scratch_shapes=[pltpu.VMEM((HDIM, block_rows), F32)]
            + [pltpu.VMEM((block_rows, HDIM), F32)] * 2,
        ),
        out_shape=[dq_shape] + dkv_shapes,
        compiler_params=pltpu.CompilerParams(vmem_limit_bytes=VMEM_LIMIT),
        name="attention_backward",
    )(place, query, out, grad, lse, *blocks, *([dq] if started else []))


def feed_kernel(
    normed_ref, grad_ref, both_ref, down_ref, mixed_ref, back_ref, out_ref, *, columns
):
    hidden = down_ref.shape[0]
    for first in range(0, hidden, columns):
        gates = slice(first, first + columns)
        ups = slice(hidden + first, hidden + first + columns)
        gate_act = dot(normed_ref[...], both_ref[:, gates])
        up_act = dot(normed_ref[...], both_ref[:, ups])
        mixed_grad = dot_transposed(grad_ref[...], down_ref[gates, :])
        sigmoid_gate = 1.0 / (1.0 + jnp.exp(-gate_act))
        silu_gate = gate_act * sigmoid_gate
        mixed_ref[:, gates] = (silu_gate * up_act).astype(BF16)
        slope = sigmoid_gate * (1.0 + gate_act * (1.0 - sigmoid_gate))
        back_ref[:, gates] = (mixed_grad * up_act * slope).astype(BF16)
        back_ref[:, ups] = (mixed_grad * silu_gate).astype(BF16)
    out_ref[...] = dot_transposed(back_ref[...], both_ref[...]).astype(BF16)


def feed_forward(normed, grad, both, down):
    rows, width = normed.shape
    hidden = down.shape[0]
    tile = min(256, rows)

    def by_rows(columns):
        return pl.BlockSpec((tile, columns), lambda i: (i, 0))

    def whole(array):
        return pl.BlockSpec(array.shape, lambda i: (0, 0), pipeline_mode=pl.Buffered(1))

    return pl.pallas_call(
        functools.partial(feed_kernel, columns=min(256, hidden)),
        grid=(rows // tile,),
        in_specs=[by_rows(width), by_rows(width), whole(both), whole(down)],
        out_specs=[by_rows(hidden), by_rows(2 * hidden), by_rows(width)],
        out_shape=[
            jax.ShapeDtypeStruct((rows, hidden), BF16),
            jax.ShapeDtypeStruct((rows, 2 * hidden), BF16),
            jax.ShapeDtypeStruct((rows, width), BF16),
        ],
        compiler_params=pltpu.CompilerParams(vmem_limit_bytes=VMEM_LIMIT),
        name="feed_forward",
    )(normed, grad, both, down)


def local(
    tokens,
    lengths,
    query_weight,
    key_weight,
    value_weight,
    output_weight,
    gate_weight,
    up_weight,
    down_weight,
    cotangent,
):
    blocks = lax.axis_size("blk")
    parts = lax.axis_size("head")
    me = lax.axis_index("blk")
    part = lax.axis_index("head")
    inputs = tokens[0].astype(F32)
    token_count, model_width = inputs.shape
    hidden_width = gate_weight.shape[1]
    heads = HEADS // parts
    width = heads * HDIM
    block_rows = SEQ // blocks
    group_rows = token_count * parts
    slots = group_rows // block_rows
    shard_rows = query_weight.shape[0]
    band_rows = shard_rows * parts
    chunk = hidden_width // (blocks * parts)
    masks = list(range(blocks))
    place = jnp.concatenate([me[None].astype(jnp.int32), lengths.astype(jnp.int32)])

    row_ids = part * token_count + jnp.arange(token_count)
    my_length = jnp.sum(
        jnp.where((row_ids // block_rows)[:, None] == jnp.arange(slots)[None, :], lengths[None, :], 0),
        axis=1,
    )
    valid = (me * block_rows + row_ids % block_rows < my_length).astype(F32)[:, None]

    normed_one = normalize_rows(inputs)[0]
    with jax.named_scope("projection_weights"):
        stacked = collect([query_weight, key_weight, value_weight], parts, 1, width)
        stacked = lax.all_to_all(stacked, "head", split_axis=0, concat_axis=0, tiled=True)
        stacked = stacked.reshape(band_rows, 3 * width)
        normed_start = after(normed_one.astype(BF16), stacked)
        near = send_near(stacked)
        far = send_far(near)
        projection = gather_blk(stacked, near + far).reshape(model_width, 3 * width)

    with jax.named_scope("tokens_gather"):
        upstream_low = (cotangent[0].astype(F32) * valid).astype(BF16)
        normed_group = lax.all_gather(
            normed_start, "head", axis=0, tiled=True
        )

    with jax.named_scope("hidden_weights"):
        gate = collect([gate_weight], parts, blocks, chunk)
        up = collect([up_weight], parts, blocks, chunk)
        output_rows = lax.ppermute(
            after(output_weight, stacked),
            ("blk", "head"),
            [(h * blocks + b, b * parts + h) for b in range(blocks) for h in range(parts)],
        )
        output_rows = after(output_rows, far)
        output_near = send_near(output_rows)
        output = gather_blk(output_rows, output_near + send_far(output_near))
        output = output.reshape(width, model_width)
        normed_group, projection, output = lax.optimization_barrier(
            (normed_group, projection, output)
        )

    cosine, sine = rotary_tables(me * block_rows + jnp.arange(block_rows))
    with jax.named_scope("projections"):
        query, key_value = project(normed_group, projection, cosine, sine, heads, block_rows)

    with jax.named_scope("attention"):
        sent = [swapped(key_value, mask, lambda i, j: j > i) for mask in masks[1:]]
        upstream_group = lax.all_gather(
            after(upstream_low, normed_group), "head", axis=0, tiled=True
        )
        gate = lax.all_to_all(
            after(gate, query), "head", split_axis=0, concat_axis=0, tiled=True
        )
        sent, gate = lax.optimization_barrier((sent, gate))
        up = lax.all_to_all(
            after(up, upstream_group, *sent), "head", split_axis=0, concat_axis=0, tiled=True
        )
        attended, log_total = forward_attention(
            place, query, [key_value] + sent, masks, None, True, heads, block_rows
        )
        down_near = send_near(after(down_weight, sent[0]))
        joined_partial = dot(after(attended, down_near), output).astype(BF16)
        joined_partial, down_near, up = lax.optimization_barrier(
            (joined_partial, down_near, up)
        )
        both = jnp.concatenate([gate, up], axis=2).reshape(band_rows, 2 * blocks * chunk)
        near = send_near(both)
        joined = lax.psum_scatter(joined_partial, "head", scatter_dimension=0, tiled=True)
        joined, near = lax.optimization_barrier((joined, near))
        near, far = lax.optimization_barrier((near, send_far(near)))
        both = gather_blk(both, near + far).reshape(model_width, 2 * blocks * chunk)
        down_near = after(down_near, far)
        down_near, down_far = lax.optimization_barrier((down_near, send_far(down_near)))
        down = gather_blk(down_weight, down_near + down_far).reshape(blocks * chunk, model_width)

    with jax.named_scope("feed_forward"):
        residual, normed_two = add_and_norm(tokens[0], joined)
        normed_two_group = lax.all_gather(normed_two, "head", axis=0, tiled=True)
        mixed, both_back, normed_two_partial = feed_forward(
            normed_two_group, upstream_group, both, down
        )
        normed_two_grad = lax.psum_scatter(
            normed_two_partial, "head", scatter_dimension=0, tiled=True
        )
        down_partial = dot(mixed, down).astype(BF16)

        def band(values, place_of):
            return lax.dynamic_slice_in_dim(values, place_of * band_rows, band_rows, 1)

        both_terms = terms_of(lambda j: outer_sum(band(normed_two_group, j), both_back))
        both_passed = sum_pass(both_terms)
        down_terms = terms_of(
            lambda j: outer_sum(lax.dynamic_slice_in_dim(mixed, j * chunk, chunk, 1), upstream_group)
        )
        normed_two_grad, down_partial, both_terms, both_passed, down_terms = (
            lax.optimization_barrier(
                (normed_two_grad, down_partial, both_terms, both_passed, down_terms)
            )
        )

    residual_grad, residual_low = norm_back(residual, upstream_low, normed_two_grad, (F32, BF16))

    def to_shards(summed):
        return lax.all_to_all(
            summed.astype(BF16).reshape(parts, shard_rows, summed.shape[1]),
            "head",
            split_axis=0,
            concat_axis=0,
            tiled=True,
        )

    with jax.named_scope("attention_back"):
        residual_group = lax.all_gather(residual_low, "head", axis=0, tiled=True)
        both_own, both_far = sum_own(both_terms), sum_far(both_terms, both_passed)
        both_sum = sum_end(both_terms, both_own, both_far).astype(BF16)
        residual_group, both_sum, down_terms = lax.optimization_barrier(
            (residual_group, both_sum, down_terms)
        )
        down_passed, down_own = sum_pass(down_terms), sum_own(down_terms)
        attended_grad = dot_transposed(residual_group, output).astype(BF16)
        down_act = lax.psum_scatter(
            after(down_partial, residual_group), "head", scatter_dimension=0, tiled=True
        ).astype(F32)
        order = masks[:0:-1] + [0]
        query_grad, *pairs = backward_attention(
            place, query, [([key_value] + sent)[mask] for mask in order], order, attended,
            attended_grad, log_total, None, True, heads, block_rows,
        )
        key_value_grads = [pairs[-1]] + [
            swapped(pairs[order.index(mask)], mask, lambda i, j: j < i) for mask in masks[1:]
        ]
        query_grad, both_sum, down_passed, down_own = lax.optimization_barrier(
            (query_grad, both_sum, down_passed, down_own)
        )
        hidden_shards = to_shards(both_sum)
        residual_group = after(residual_group, key_value_grads[1])
        output_terms = terms_of(
            lambda j: outer_sum(
                lax.dynamic_slice_in_dim(attended, j * shard_rows, shard_rows, 1), residual_group
            )
        )
        query_grad, key_value_grads, hidden_shards, output_terms = lax.optimization_barrier(
            (query_grad, key_value_grads, hidden_shards, output_terms)
        )
        down_act = after(down_act, query_grad)
        layer_output = ((residual + down_act) * valid).astype(BF16)[None]
        projection_back, normed_one_partial = project_back(
            place,
            pltpu.with_memory_space_constraint(query_grad, pltpu.HBM),
            projection,
            cosine,
            sine,
            [pltpu.with_memory_space_constraint(part, pltpu.HBM) for part in key_value_grads],
            masks,
            heads,
            block_rows,
        )
        normed_one_grad = lax.psum_scatter(
            normed_one_partial, "head", scatter_dimension=0, tiled=True
        )
        (tokens_grad,) = norm_back(tokens[0], residual_grad, normed_one_grad, (BF16,))
        tokens_grad = tokens_grad[None]

    with jax.named_scope("weight_grads"):

        gate_grad, up_grad = spread(hidden_shards, 2, parts, blocks, chunk)
        terms = terms_of(lambda j: outer_sum(band(normed_group, j), projection_back))
        passed, own = sum_pass(terms), sum_own(terms)
        passed, own, terms, output_terms, gate_grad, up_grad = lax.optimization_barrier(
            (passed, own, terms, output_terms, gate_grad, up_grad)
        )
        summed = sum_end(terms, own, sum_far(terms, passed))
        summed, output_part, down_passed = lax.optimization_barrier(
            (summed, sum_to_owner(output_terms), down_passed)
        )
        down_sum = sum_end(down_terms, down_own, sum_far(down_terms, down_passed))
        output_grad = lax.ppermute(
            output_part.astype(BF16),
            ("blk", "head"),
            [(b * parts + h, h * blocks + b) for b in range(blocks) for h in range(parts)],
        )
        shards, output_grad, tokens_grad = lax.optimization_barrier(
            (to_shards(summed), output_grad, tokens_grad)
        )
        output_grad = output_grad.astype(F32)
        projection_grads = spread(shards, 3, parts, 1, width)
    return (
        layer_output,
        tokens_grad,
        projection_grads[0],
        projection_grads[1],
        projection_grads[2],
        output_grad,
        gate_grad,
        up_grad,
        down_sum,
    )


def solution(mesh):
    rows = P(("blk", "head"), None)
    places = P("blk", "head", None)
    in_specs = (places, P(), rows, rows, rows, rows, rows, rows, rows, places)
    out_specs = (places, places, rows, rows, rows, rows, rows, rows, rows)
    return jax.shard_map(local, mesh=mesh, in_specs=in_specs, out_specs=out_specs, check_vma=False)
```

```python
import functools
import math

import jax
import jax.numpy as jnp
from jax import lax
from jax.experimental import pallas as pl
from jax.experimental.pallas import tpu as pltpu
from jax.sharding import PartitionSpec as P

HEADS = 16
HDIM = 128
SEQ = 4096

EPSILON = 1e-05
NEGATIVE = -1e30
SCALE = 1.0 / math.sqrt(HDIM)
SCALE2 = SCALE * math.log2(math.e)
TILE = 512
VMEM_LIMIT = 48 * 1024 * 1024
BF16 = jnp.bfloat16
F32 = jnp.float32


def normalize_rows(values):
    centered = values - jnp.mean(values, axis=-1, keepdims=True)
    variance = jnp.mean(centered * centered, axis=-1, keepdims=True)
    inverse = lax.rsqrt(variance + EPSILON)
    return (centered * inverse, inverse)


def normalize_back(normed, inverse, upstream):
    mean_grad = jnp.mean(upstream, axis=-1, keepdims=True)
    mean_proj = jnp.mean(upstream * normed, axis=-1, keepdims=True)
    return inverse * (upstream - mean_grad - normed * mean_proj)


def rotary_tables(positions):
    half_dim = HDIM // 2
    frequency = jnp.exp(
        jnp.arange(half_dim).astype(F32) * (-2.0 * math.log(10000.0) / HDIM)
    )
    angles = positions.astype(F32)[:, None] * frequency[None, :]
    cosine, sine = jnp.cos(angles), jnp.sin(angles)
    return (
        jnp.concatenate([cosine, cosine], axis=1),
        jnp.concatenate([-sine, sine], axis=1),
    )


def dot(left, right):
    return jnp.dot(left, right, preferred_element_type=F32)


def dot_transposed(left, right):
    return lax.dot_general(left, right, (((1,), (1,)), ((), ())), preferred_element_type=F32)


def outer_sum(left, right):
    return lax.dot_general(left, right, (((0,), (0,)), ((), ())), preferred_element_type=F32)


def swapped(value, mask, keep=None):
    peers = lax.axis_size("blk")
    pairs = [(i, i ^ mask) for i in range(peers) if keep is None or keep(i, i ^ mask)]
    return lax.ppermute(value, "blk", pairs)


def after(value, *others):
    return lax.optimization_barrier((value,) + others)[0]


def send_near(value):
    peers = lax.axis_size("blk")
    return [swapped(value, mask) for mask in range(1, 3 if peers == 4 else peers)]


def send_far(near):
    if lax.axis_size("blk") != 4:
        return []
    first, second = near
    half = first.shape[0] // 2
    return [[swapped(first[:half], 2), swapped(second[half:], 1)]]


def gather_blk(value, arrived):
    peers = lax.axis_size("blk")
    me = lax.axis_index("blk")
    whole = jnp.zeros((peers,) + value.shape, value.dtype)
    whole = lax.dynamic_update_index_in_dim(whole, value, me, 0)
    for mask, part in enumerate(arrived, 1):
        row = 0
        for piece in part if isinstance(part, list) else [part]:
            start = (me ^ mask, row) + (0,) * (value.ndim - 1)
            whole = lax.dynamic_update_slice(whole, piece[None], start)
            row += piece.shape[0]
    return whole


def terms_of(part_for):
    peers = lax.axis_size("blk")
    me = lax.axis_index("blk")
    return [part_for(me)] + [part_for(me ^ mask).astype(BF16) for mask in range(1, peers)]


def near_halves(terms):
    half = terms[0].shape[0] // 2
    return ((slice(0, half), 1, 2), (slice(half, None), 2, 1))


def sum_pass(terms):
    if len(terms) != 4:
        return []
    return [swapped(terms[3][rows], near) for rows, near, _ in near_halves(terms)]


def sum_own(terms):
    if len(terms) != 4:
        return [swapped(term, mask) for mask, term in enumerate(terms) if mask]
    return [swapped(terms[near][rows], near) for rows, near, _ in near_halves(terms)]


def sum_passing(terms, passed):
    return [
        (terms[far][rows].astype(F32) + part.astype(F32)).astype(BF16)
        for part, (rows, _, far) in zip(passed, near_halves(terms))
    ]


def send_passing(passing):
    return [swapped(part, far) for part, far in zip(passing, (2, 1))]


def sum_far(terms, passed):
    return send_passing(sum_passing(terms, passed))


def sum_end(terms, own, far):
    total = terms[0]
    if len(terms) != 4:
        for part in own:
            total = total + part.astype(F32)
        return total
    totals = [
        total[rows] + first.astype(F32) + second.astype(F32)
        for first, second, (rows, _, _) in zip(own, far, near_halves(terms))
    ]
    return jnp.concatenate(totals, axis=0)


def sum_to_owner(terms):
    arrived = [swapped(term, mask) for mask, term in enumerate(terms) if mask]
    total = terms[0]
    for part in arrived:
        total = total + part.astype(F32)
    return total


def collect_kernel(*refs, parts, blocks, chunk):
    *ins, out_ref = refs
    for number, ref in enumerate(ins):
        for block in range(blocks):
            first = (number * blocks + block) * chunk
            for part in range(parts):
                start = (block * parts + part) * chunk
                out_ref[part, :, first : first + chunk] = ref[:, start : start + chunk]


def collect(arrays, parts, blocks, chunk):
    rows = arrays[0].shape[0]
    return pl.pallas_call(
        functools.partial(collect_kernel, parts=parts, blocks=blocks, chunk=chunk),
        out_shape=jax.ShapeDtypeStruct(
            (parts, rows, len(arrays) * blocks * chunk), arrays[0].dtype
        ),
        compiler_params=pltpu.CompilerParams(vmem_limit_bytes=VMEM_LIMIT),
        name="collect",
    )(*arrays)


def spread_kernel(in_ref, *outs, parts, blocks, chunk):
    for number, ref in enumerate(outs):
        for block in range(blocks):
            first = (number * blocks + block) * chunk
            for part in range(parts):
                start = (block * parts + part) * chunk
                ref[:, start : start + chunk] = in_ref[part, :, first : first + chunk].astype(F32)


def spread(array, count, parts, blocks, chunk):
    rows = array.shape[1]
    shape = jax.ShapeDtypeStruct((rows, blocks * parts * chunk), F32)
    return pl.pallas_call(
        functools.partial(spread_kernel, parts=parts, blocks=blocks, chunk=chunk),
        out_shape=[shape] * count,
        compiler_params=pltpu.CompilerParams(vmem_limit_bytes=VMEM_LIMIT),
        name="spread",
    )(array)


def project_kernel(normed_ref, weight_ref, cos_ref, sin_ref, q_ref, kv_ref, *, heads):
    cosine, sine = cos_ref[...], sin_ref[...]
    linear = dot(normed_ref[...], weight_ref[...]).astype(BF16)
    for part in range(2 * heads):
        value = linear[:, part * HDIM : (part + 1) * HDIM].astype(F32)
        turned = (value * cosine + pltpu.roll(value, HDIM // 2, 1) * sine).astype(BF16)
        if part < heads:
            q_ref[:, part * HDIM : (part + 1) * HDIM] = turned
        else:
            start = 2 * (part - heads) * HDIM
            kv_ref[:, start : start + HDIM] = turned
            first = (part + heads) * HDIM
            kv_ref[:, start + HDIM : start + 2 * HDIM] = linear[:, first : first + HDIM]


def project(normed, weight, cosine, sine, heads, block_rows):
    rows, model_width = normed.shape
    width = heads * HDIM
    tile = min(256, block_rows)
    per_block = block_rows // tile
    return pl.pallas_call(
        functools.partial(project_kernel, heads=heads),
        grid=(rows // tile,),
        in_specs=[
            pl.BlockSpec((tile, model_width), lambda i: (i, 0)),
            pl.BlockSpec(weight.shape, lambda i: (0, 0), pipeline_mode=pl.Buffered(1)),
            pl.BlockSpec((tile, HDIM), lambda i: (i % per_block, 0)),
            pl.BlockSpec((tile, HDIM), lambda i: (i % per_block, 0)),
        ],
        out_specs=[
            pl.BlockSpec((tile, width), lambda i: (i, 0)),
            pl.BlockSpec((tile, 2 * width), lambda i: (i, 0)),
        ],
        out_shape=[
            jax.ShapeDtypeStruct((rows, width), BF16),
            jax.ShapeDtypeStruct((rows, 2 * width), BF16),
        ],
        compiler_params=pltpu.CompilerParams(vmem_limit_bytes=VMEM_LIMIT),
        name="project",
    )(normed, weight, cosine, sine)


def project_back_kernel(
    place_ref, dq_ref, weight_ref, cos_ref, sin_ref, *refs, heads, masks
):
    parts, out_ref, sum_ref = refs[:-2], refs[-2], refs[-1]
    width = heads * HDIM
    me = place_ref[0]
    cosine, sine = cos_ref[...], sin_ref[...]

    def back(value):
        return (value * cosine - pltpu.roll(value, HDIM // 2, 1) * sine).astype(BF16)

    for head in range(heads):
        columns = slice(head * HDIM, (head + 1) * HDIM)
        out_ref[:, columns] = back(dq_ref[:, columns])
    for part in range(2 * heads):
        head, is_value = part // 2, part % 2
        columns = slice(part * HDIM, (part + 1) * HDIM)
        total = parts[0][:, columns].astype(F32)
        for mask, ref in zip(masks[1:], parts[1:]):
            total = total + jnp.where((me ^ mask) > me, ref[:, columns].astype(F32), 0.0)
        start = (1 + is_value) * width + head * HDIM
        out_ref[:, start : start + HDIM] = total.astype(BF16) if is_value else back(total)
    sum_ref[...] = dot_transposed(out_ref[...], weight_ref[...]).astype(BF16)


def project_back(place, dq, weight, cosine, sine, parts, masks, heads, block_rows):
    rows = dq.shape[0]
    width = heads * HDIM
    model_width = weight.shape[0]
    tile = min(256, block_rows)
    per_block = block_rows // tile
    return pl.pallas_call(
        functools.partial(project_back_kernel, heads=heads, masks=masks),
        grid_spec=pltpu.PrefetchScalarGridSpec(
            num_scalar_prefetch=1,
            grid=(rows // tile,),
            in_specs=[
                pl.BlockSpec((tile, width), lambda i, *_: (i, 0)),
                pl.BlockSpec(weight.shape, lambda i, *_: (0, 0), pipeline_mode=pl.Buffered(1)),
                pl.BlockSpec((tile, HDIM), lambda i, *_: (i % per_block, 0)),
                pl.BlockSpec((tile, HDIM), lambda i, *_: (i % per_block, 0)),
            ]
            + [pl.BlockSpec((tile, 2 * width), lambda i, *_: (i, 0))] * len(parts),
            out_specs=[
                pl.BlockSpec((tile, 3 * width), lambda i, *_: (i, 0)),
                pl.BlockSpec((tile, model_width), lambda i, *_: (i, 0)),
            ],
        ),
        out_shape=[
            jax.ShapeDtypeStruct((rows, 3 * width), BF16),
            jax.ShapeDtypeStruct((rows, model_width), BF16),
        ],
        compiler_params=pltpu.CompilerParams(vmem_limit_bytes=VMEM_LIMIT),
        name="project_back",
    )(place, dq, weight, cosine, sine, *parts)


def norm_kernel(in_ref, part_ref, sum_ref, low_ref):
    total = in_ref[...].astype(F32) + part_ref[...].astype(F32)
    sum_ref[...] = total
    low_ref[...] = normalize_rows(total)[0].astype(BF16)


def add_and_norm(inputs, part):
    rows, width = inputs.shape
    tile = min(64, rows)
    spec = pl.BlockSpec((tile, width), lambda i: (i, 0))
    return pl.pallas_call(
        norm_kernel,
        grid=(rows // tile,),
        in_specs=[spec] * 2,
        out_specs=[spec] * 2,
        out_shape=[
            jax.ShapeDtypeStruct((rows, width), F32),
            jax.ShapeDtypeStruct((rows, width), BF16),
        ],
        compiler_params=pltpu.CompilerParams(vmem_limit_bytes=VMEM_LIMIT),
        name="add_and_norm",
    )(inputs, part)


def norm_back_kernel(in_ref, upstream_ref, grad_ref, *out_refs):
    normed, inverse = normalize_rows(in_ref[...].astype(F32))
    total = upstream_ref[...].astype(F32) + normalize_back(
        normed, inverse, grad_ref[...].astype(F32)
    )
    for ref in out_refs:
        ref[...] = total.astype(ref.dtype)


def norm_back(values, upstream, grad, dtypes):
    rows, width = values.shape
    tile = min(64, rows)
    spec = pl.BlockSpec((tile, width), lambda i: (i, 0))
    return pl.pallas_call(
        norm_back_kernel,
        grid=(rows // tile,),
        in_specs=[spec] * 3,
        out_specs=[spec] * len(dtypes),
        out_shape=[jax.ShapeDtypeStruct((rows, width), dtype) for dtype in dtypes],
        compiler_params=pltpu.CompilerParams(vmem_limit_bytes=VMEM_LIMIT),
        name="norm_back",
    )(values, upstream, grad)


def visible(first_row, rows, first_key, keys, length):
    row = first_row + lax.broadcasted_iota(jnp.int32, (keys, rows), 1)
    key = first_key + lax.broadcasted_iota(jnp.int32, (keys, rows), 0)
    return (key <= row) & (key < length)

def block_cases(place_ref, mask, block_rows, body):
    me = place_ref[0]
    length = place_ref[1 + pl.program_id(0)]
    if mask == 0:
        body(True, True, me, length)
        return
    source = me ^ mask
    whole = (source + 1) * block_rows <= length
    @pl.when((source < me) & whole)
    def _():
        body(False, False, source, length)
    @pl.when((source < me) & jnp.logical_not(whole))
    def _():
        body(False, True, source, length)

def forward_kernel(place_ref, q_ref, *refs, masks, started, final, tile, block_rows):
    kv_refs, refs = refs[: len(masks)], refs[len(masks) :]
    if started:
        (m_in, l_in, acc_in), refs = refs[:3], refs[3:]
    outs, (m_ref, l_ref, acc_ref) = refs[:-3], refs[-3:]
    if started:
        m_ref[...] = m_in[0]
        l_ref[...] = l_in[0]
        acc_ref[...] = acc_in[0]
    else:
        m_ref[...] = jnp.full(m_ref.shape, NEGATIVE, F32)
        l_ref[...] = jnp.zeros(l_ref.shape, F32)
        acc_ref[...] = jnp.zeros(acc_ref.shape, F32)
    me = place_ref[0]
    for mask, kv_ref in zip(masks, kv_refs):

        def body(diagonal, masked, source, length, kv_ref=kv_ref):
            for first in range(0, block_rows, tile):
                rows = slice(first, first + tile)
                keys = first + tile if diagonal else block_rows
                scores = dot_transposed(kv_ref[:keys, :HDIM], q_ref[rows, :])
                if masked:
                    seen = visible(me * block_rows + first, tile, source * block_rows, keys, length)
                    scores = jnp.where(seen, scores, NEGATIVE)
                peak_old = m_ref[:, rows]
                peak = jnp.maximum(peak_old, jnp.max(scores, axis=0, keepdims=True) * SCALE2)
                shrink = jnp.exp2(peak_old - peak)
                weights = jnp.exp2(scores * SCALE2 - peak)
                l_ref[:, rows] = l_ref[:, rows] * shrink + jnp.sum(weights, axis=0, keepdims=True)
                acc_ref[:, rows] = acc_ref[:, rows] * shrink + outer_sum(
                    kv_ref[:keys, HDIM:], weights.astype(BF16)
                )
                m_ref[:, rows] = peak
        block_cases(place_ref, mask, block_rows, body)
    if final:
        o_ref, lse_ref = outs
        total = l_ref[...]
        o_ref[...] = (acc_ref[...] / total).T.astype(BF16)
        lse_ref[0] = m_ref[...] + jnp.log2(total)
    else:
        for out, ref in zip(outs, (m_ref, l_ref, acc_ref)):
            out[0] = ref[...]

def forward_attention(place, query, blocks, masks, state, final, heads, block_rows):
    rows, width = query.shape
    groups = rows // block_rows * heads
    head_block = pl.BlockSpec((block_rows, HDIM), lambda s, n, *_: (s, n))
    pair_block = pl.BlockSpec((block_rows, 2 * HDIM), lambda s, n, *_: (s, n))
    row_block = pl.BlockSpec((1, 1, block_rows), lambda s, n, *_: (s * heads + n, 0, 0))
    acc_block = pl.BlockSpec((1, HDIM, block_rows), lambda s, n, *_: (s * heads + n, 0, 0))
    row_shape = jax.ShapeDtypeStruct((groups, 1, block_rows), F32)
    acc_shape = jax.ShapeDtypeStruct((groups, HDIM, block_rows), F32)
    if final:
        out_specs, out_shape = [head_block, row_block], [jax.ShapeDtypeStruct((rows, width), BF16), row_shape]
    else:
        out_specs, out_shape = [row_block, row_block, acc_block], [row_shape, row_shape, acc_shape]
    started = state is not None
    operands = [query, *blocks] + (list(state) if started else [])
    return pl.pallas_call(
        functools.partial(forward_kernel, masks=masks, started=started, final=final, tile=min(TILE, block_rows), block_rows=block_rows),
        grid_spec=pltpu.PrefetchScalarGridSpec(
            num_scalar_prefetch=1, grid=(rows // block_rows, heads),
            in_specs=[head_block] + [pair_block] * len(blocks) + ([row_block, row_block, acc_block] if started else []),
            out_specs=out_specs,
            scratch_shapes=[pltpu.VMEM((1, block_rows), F32)] * 2 + [pltpu.VMEM((HDIM, block_rows), F32)],
        ),
        out_shape=out_shape,
        compiler_params=pltpu.CompilerParams(vmem_limit_bytes=VMEM_LIMIT),
        name="attention_forward",
    )(place, *operands)

def backward_kernel(
    place_ref, q_ref, o_ref, do_ref, lse_ref, *refs, masks, started, final, tile, block_rows
):
    kv_refs, refs = refs[: len(masks)], refs[len(masks) :]
    if started:
        dq_in, refs = refs[0], refs[1:]
    dq_ref, dkv_refs, (dq_acc, dk_acc, dv_acc) = refs[0], refs[1:-3], refs[-3:]
    dq_acc[...] = dq_in[0] if started else jnp.zeros(dq_acc.shape, F32)
    me = place_ref[0]
    for mask, kv_ref, dkv_ref in zip(masks, kv_refs, dkv_refs):

        def body(diagonal, masked, source, length, kv_ref=kv_ref, dkv_ref=dkv_ref):
            for first in range(0, block_rows, tile):
                rows = slice(first, first + tile)
                keys = first + tile if diagonal else block_rows
                query, grad = q_ref[rows, :], do_ref[rows, :]
                key, value = kv_ref[:keys, :HDIM], kv_ref[:keys, HDIM:]
                delta = jnp.sum(
                    (grad.astype(F32) * o_ref[rows, :].astype(F32)).T, axis=0, keepdims=True
                )
                scores = dot_transposed(key, query)
                if masked:
                    seen = visible(
                        me * block_rows + first, tile, source * block_rows, keys, length
                    )
                    scores = jnp.where(seen, scores, NEGATIVE)
                probs = jnp.exp2(scores * SCALE2 - lse_ref[0, :, rows])
                prob_grad = dot_transposed(value, grad)
                score_grad = (probs * (prob_grad - delta)).astype(BF16)
                dv = dot(probs.astype(BF16), grad)
                dk = dot(score_grad, query)
                dq_acc[:, rows] += outer_sum(key, score_grad) * SCALE
                if diagonal:
                    if first:
                        dk_acc[:first, :] += dk[:first]
                        dv_acc[:first, :] += dv[:first]
                    dk_acc[rows, :] = dk[first:]
                    dv_acc[rows, :] = dv[first:]
                elif first == 0:
                    dk_acc[...] = dk
                    dv_acc[...] = dv
                else:
                    dk_acc[...] += dk
                    dv_acc[...] += dv
            dkv_ref[:, :HDIM] = (dk_acc[...] * SCALE).astype(BF16)
            dkv_ref[:, HDIM:] = dv_acc[...].astype(BF16)

        block_cases(place_ref, mask, block_rows, body)
    if final:
        dq_ref[...] = dq_acc[...].T
    else:
        dq_ref[0] = dq_acc[...]


def backward_attention(
    place, query, blocks, masks, out, grad, lse, dq, final, heads, block_rows
):
    rows, width = query.shape
    groups = rows // block_rows * heads
    head_block = pl.BlockSpec((block_rows, HDIM), lambda s, n, *_: (s, n))
    pair_block = pl.BlockSpec((block_rows, 2 * HDIM), lambda s, n, *_: (s, n))
    row_block = pl.BlockSpec((1, 1, block_rows), lambda s, n, *_: (s * heads + n, 0, 0))
    acc_block = pl.BlockSpec((1, HDIM, block_rows), lambda s, n, *_: (s * heads + n, 0, 0))
    started = dq is not None
    if final:
        dq_shape = jax.ShapeDtypeStruct((rows, width), F32)
    else:
        dq_shape = jax.ShapeDtypeStruct((groups, HDIM, block_rows), F32)
    dkv_shapes = [
        pltpu.HBM((rows, 2 * width), BF16) if mask else jax.ShapeDtypeStruct((rows, 2 * width), BF16)
        for mask in masks
    ]
    return pl.pallas_call(
        functools.partial(
            backward_kernel,
            masks=masks,
            started=started,
            final=final,
            tile=min(TILE, block_rows),
            block_rows=block_rows,
        ),
        grid_spec=pltpu.PrefetchScalarGridSpec(
            num_scalar_prefetch=1,
            grid=(rows // block_rows, heads),
            in_specs=[head_block] * 3
            + [row_block]
            + [pair_block] * len(masks)
            + ([acc_block] if started else []),
            out_specs=[head_block if final else acc_block] + [pair_block] * len(masks),
            scratch_shapes=[pltpu.VMEM((HDIM, block_rows), F32)]
            + [pltpu.VMEM((block_rows, HDIM), F32)] * 2,
        ),
        out_shape=[dq_shape] + dkv_shapes,
        compiler_params=pltpu.CompilerParams(vmem_limit_bytes=VMEM_LIMIT),
        name="attention_backward",
    )(place, query, out, grad, lse, *blocks, *([dq] if started else []))


def feed_kernel(
    normed_ref, grad_ref, both_ref, down_ref, mixed_ref, back_ref, out_ref, *, columns
):
    hidden = down_ref.shape[0]
    for first in range(0, hidden, columns):
        gates = slice(first, first + columns)
        ups = slice(hidden + first, hidden + first + columns)
        gate_act = dot(normed_ref[...], both_ref[:, gates])
        up_act = dot(normed_ref[...], both_ref[:, ups])
        mixed_grad = dot_transposed(grad_ref[...], down_ref[gates, :])
        sigmoid_gate = 1.0 / (1.0 + jnp.exp(-gate_act))
        silu_gate = gate_act * sigmoid_gate
        mixed_ref[:, gates] = (silu_gate * up_act).astype(BF16)
        slope = sigmoid_gate * (1.0 + gate_act * (1.0 - sigmoid_gate))
        back_ref[:, gates] = (mixed_grad * up_act * slope).astype(BF16)
        back_ref[:, ups] = (mixed_grad * silu_gate).astype(BF16)
    out_ref[...] = dot_transposed(back_ref[...], both_ref[...]).astype(BF16)


def feed_forward(normed, grad, both, down):
    rows, width = normed.shape
    hidden = down.shape[0]
    tile = min(256, rows)

    def by_rows(columns):
        return pl.BlockSpec((tile, columns), lambda i: (i, 0))

    def whole(array):
        return pl.BlockSpec(array.shape, lambda i: (0, 0), pipeline_mode=pl.Buffered(1))

    return pl.pallas_call(
        functools.partial(feed_kernel, columns=min(256, hidden)),
        grid=(rows // tile,),
        in_specs=[by_rows(width), by_rows(width), whole(both), whole(down)],
        out_specs=[by_rows(hidden), by_rows(2 * hidden), by_rows(width)],
        out_shape=[
            jax.ShapeDtypeStruct((rows, hidden), BF16),
            jax.ShapeDtypeStruct((rows, 2 * hidden), BF16),
            jax.ShapeDtypeStruct((rows, width), BF16),
        ],
        compiler_params=pltpu.CompilerParams(vmem_limit_bytes=VMEM_LIMIT),
        name="feed_forward",
    )(normed, grad, both, down)


def local(
    tokens,
    lengths,
    query_weight,
    key_weight,
    value_weight,
    output_weight,
    gate_weight,
    up_weight,
    down_weight,
    cotangent,
):
    blocks = lax.axis_size("blk")
    parts = lax.axis_size("head")
    me = lax.axis_index("blk")
    part = lax.axis_index("head")
    inputs = tokens[0].astype(F32)
    token_count, model_width = inputs.shape
    hidden_width = gate_weight.shape[1]
    heads = HEADS // parts
    width = heads * HDIM
    block_rows = SEQ // blocks
    group_rows = token_count * parts
    slots = group_rows // block_rows
    shard_rows = query_weight.shape[0]
    band_rows = shard_rows * parts
    chunk = hidden_width // (blocks * parts)
    masks = list(range(blocks))
    place = jnp.concatenate([me[None].astype(jnp.int32), lengths.astype(jnp.int32)])

    row_ids = part * token_count + jnp.arange(token_count)
    my_length = jnp.sum(
        jnp.where((row_ids // block_rows)[:, None] == jnp.arange(slots)[None, :], lengths[None, :], 0),
        axis=1,
    )
    valid = (me * block_rows + row_ids % block_rows < my_length).astype(F32)[:, None]

    normed_one = normalize_rows(inputs)[0]
    with jax.named_scope("projection_weights"):
        stacked = collect([query_weight, key_weight, value_weight], parts, 1, width)
        stacked = lax.all_to_all(stacked, "head", split_axis=0, concat_axis=0, tiled=True)
        stacked = stacked.reshape(band_rows, 3 * width)
        normed_start = after(normed_one.astype(BF16), stacked)
        near = send_near(stacked)
        far = send_far(near)
        projection = gather_blk(stacked, near + far).reshape(model_width, 3 * width)

    with jax.named_scope("tokens_gather"):
        upstream_low = (cotangent[0].astype(F32) * valid).astype(BF16)
        normed_group = lax.all_gather(
            normed_start, "head", axis=0, tiled=True
        )

    with jax.named_scope("hidden_weights"):
        gate = collect([gate_weight], parts, blocks, chunk)
        up = collect([up_weight], parts, blocks, chunk)
        output_rows = lax.ppermute(
            after(output_weight, stacked),
            ("blk", "head"),
            [(h * blocks + b, b * parts + h) for b in range(blocks) for h in range(parts)],
        )
        output_rows = after(output_rows, far)
        output_near = send_near(output_rows)
        output = gather_blk(output_rows, output_near + send_far(output_near))
        output = output.reshape(width, model_width)
        normed_group, projection, output = lax.optimization_barrier(
            (normed_group, projection, output)
        )

    cosine, sine = rotary_tables(me * block_rows + jnp.arange(block_rows))
    with jax.named_scope("projections"):
        query, key_value = project(normed_group, projection, cosine, sine, heads, block_rows)

    with jax.named_scope("attention"):
        sent = [swapped(key_value, mask, lambda i, j: j > i) for mask in masks[1:]]
        upstream_group = lax.all_gather(
            after(upstream_low, normed_group), "head", axis=0, tiled=True
        )
        gate = lax.all_to_all(
            after(gate, query), "head", split_axis=0, concat_axis=0, tiled=True
        )
        sent, gate = lax.optimization_barrier((sent, gate))
        up = lax.all_to_all(
            after(up, upstream_group, *sent), "head", split_axis=0, concat_axis=0, tiled=True
        )
        attended, log_total = forward_attention(
            place, query, [key_value] + sent, masks, None, True, heads, block_rows
        )
        down_near = send_near(after(down_weight, sent[0]))
        joined_partial = dot(after(attended, down_near), output).astype(BF16)
        joined_partial, down_near, up = lax.optimization_barrier(
            (joined_partial, down_near, up)
        )
        both = jnp.concatenate([gate, up], axis=2).reshape(band_rows, 2 * blocks * chunk)
        near = send_near(both)
        joined = lax.psum_scatter(joined_partial, "head", scatter_dimension=0, tiled=True)
        joined, near = lax.optimization_barrier((joined, near))
        near, far = lax.optimization_barrier((near, send_far(near)))
        both = gather_blk(both, near + far).reshape(model_width, 2 * blocks * chunk)
        down_near = after(down_near, far)
        down_near, down_far = lax.optimization_barrier((down_near, send_far(down_near)))
        down = gather_blk(down_weight, down_near + down_far).reshape(blocks * chunk, model_width)

    with jax.named_scope("feed_forward"):
        residual, normed_two = add_and_norm(tokens[0], joined)
        normed_two_group = lax.all_gather(normed_two, "head", axis=0, tiled=True)
        mixed, both_back, normed_two_partial = feed_forward(
            normed_two_group, upstream_group, both, down
        )
        normed_two_grad = lax.psum_scatter(
            normed_two_partial, "head", scatter_dimension=0, tiled=True
        )
        down_partial = dot(mixed, down).astype(BF16)

        def band(values, place_of):
            return lax.dynamic_slice_in_dim(values, place_of * band_rows, band_rows, 1)

        both_terms = terms_of(lambda j: outer_sum(band(normed_two_group, j), both_back))
        both_passed = sum_pass(both_terms)
        down_terms = terms_of(
            lambda j: outer_sum(lax.dynamic_slice_in_dim(mixed, j * chunk, chunk, 1), upstream_group)
        )
        normed_two_grad, down_partial, both_terms, both_passed, down_terms = (
            lax.optimization_barrier(
                (normed_two_grad, down_partial, both_terms, both_passed, down_terms)
            )
        )

    residual_grad, residual_low = norm_back(residual, upstream_low, normed_two_grad, (F32, BF16))

    def to_shards(summed):
        return lax.all_to_all(
            summed.astype(BF16).reshape(parts, shard_rows, summed.shape[1]),
            "head",
            split_axis=0,
            concat_axis=0,
            tiled=True,
        )

    with jax.named_scope("attention_back"):
        residual_group = lax.all_gather(residual_low, "head", axis=0, tiled=True)
        both_own, both_far = sum_own(both_terms), sum_far(both_terms, both_passed)
        both_sum = sum_end(both_terms, both_own, both_far).astype(BF16)
        residual_group, both_sum, down_terms = lax.optimization_barrier(
            (residual_group, both_sum, down_terms)
        )
        down_passed, down_own = sum_pass(down_terms), sum_own(down_terms)
        attended_grad = dot_transposed(residual_group, output).astype(BF16)
        down_act = lax.psum_scatter(
            after(down_partial, residual_group), "head", scatter_dimension=0, tiled=True
        ).astype(F32)
        order = masks[:0:-1] + [0]
        query_grad, *pairs = backward_attention(
            place, query, [([key_value] + sent)[mask] for mask in order], order, attended,
            attended_grad, log_total, None, True, heads, block_rows,
        )
        key_value_grads = [pairs[-1]] + [
            swapped(pairs[order.index(mask)], mask, lambda i, j: j < i) for mask in masks[1:]
        ]
        query_grad, both_sum, down_passed, down_own = lax.optimization_barrier(
            (query_grad, both_sum, down_passed, down_own)
        )
        hidden_shards = to_shards(both_sum)
        residual_group = after(residual_group, key_value_grads[1])
        output_terms = terms_of(
            lambda j: outer_sum(
                lax.dynamic_slice_in_dim(attended, j * shard_rows, shard_rows, 1), residual_group
            )
        )
        down_passing = sum_passing(down_terms, down_passed)
        query_grad, key_value_grads, hidden_shards, output_terms, down_passing = (
            lax.optimization_barrier(
                (query_grad, key_value_grads, hidden_shards, output_terms, down_passing)
            )
        )
        down_act = after(down_act, query_grad)
        layer_output = ((residual + down_act) * valid).astype(BF16)[None]
        projection_back, normed_one_partial = project_back(
            place,
            pltpu.with_memory_space_constraint(query_grad, pltpu.HBM),
            projection,
            cosine,
            sine,
            [pltpu.with_memory_space_constraint(part, pltpu.HBM) for part in key_value_grads],
            masks,
            heads,
            block_rows,
        )
        normed_one_grad = lax.psum_scatter(
            normed_one_partial, "head", scatter_dimension=0, tiled=True
        )
        (tokens_grad,) = norm_back(tokens[0], residual_grad, normed_one_grad, (BF16,))
        tokens_grad = tokens_grad[None]

    with jax.named_scope("weight_grads"):

        gate_grad, up_grad = spread(hidden_shards, 2, parts, blocks, chunk)
        terms = terms_of(lambda j: outer_sum(band(normed_group, j), projection_back))
        passed, own = sum_pass(terms), sum_own(terms)
        passed, own, terms, output_terms, gate_grad, up_grad = lax.optimization_barrier(
            (passed, own, terms, output_terms, gate_grad, up_grad)
        )
        summed = sum_end(terms, own, sum_far(terms, passed))
        summed, output_part, down_passing = lax.optimization_barrier(
            (summed, sum_to_owner(output_terms), down_passing)
        )
        down_sum = sum_end(down_terms, down_own, send_passing(down_passing))
        output_grad = lax.ppermute(
            output_part.astype(BF16),
            ("blk", "head"),
            [(b * parts + h, h * blocks + b) for b in range(blocks) for h in range(parts)],
        )
        shards, output_grad, tokens_grad = lax.optimization_barrier(
            (to_shards(summed), output_grad, tokens_grad)
        )
        output_grad = output_grad.astype(F32)
        projection_grads = spread(shards, 3, parts, 1, width)
    return (
        layer_output,
        tokens_grad,
        projection_grads[0],
        projection_grads[1],
        projection_grads[2],
        output_grad,
        gate_grad,
        up_grad,
        down_sum,
    )


def solution(mesh):
    rows = P(("blk", "head"), None)
    places = P("blk", "head", None)
    in_specs = (places, P(), rows, rows, rows, rows, rows, rows, rows, places)
    out_specs = (places, places, rows, rows, rows, rows, rows, rows, rows)
    return jax.shard_map(local, mesh=mesh, in_specs=in_specs, out_specs=out_specs, check_vma=False)
```
